128 devices in a mesh: dp: 32 (over z, x, core), mp: 4 (over y).
Axes of the slice: x: 4, y: 4, z: 4, core: 2. Of those that a mesh axis runs over, the one named last changes fastest.
Arguments:
- candidates: int32 [512, 3], P('dp'), may hold values from 0 to 31, as said below
- row_lengths: int32 [512, 2], P('dp'), may hold values from 1 to 128
- enc_bank: bfloat16 [512, 128, 2048], P('dp', None, 'mp'), may hold values from -480 to 480
- dec_bank: bfloat16 [512, 128, 2048], P('dp', None, 'mp'), may hold values from -6 to 6
- w_query: bfloat16 [2048, 2048], P(None, 'mp'), may hold values from -0.125 to 0.125
- w_key: bfloat16 [2048, 2048], P(None, 'mp'), may hold values from -0.125 to 0.125
- w_value: bfloat16 [2048, 2048], P(None, 'mp'), may hold values from -0.125 to 0.125
Outputs:
- contexts: bfloat16 [768, 128, 2048], P('dp', None, 'mp')
The draws below stay inside these ranges and needn't reach their ends.
Inputs may be any that keep to these rules, and one draw needn't show every extreme that they name: `candidates`: row ids in columns 0 and 1 index the same shard's banks (0 to 15), column 2 is a group (0 to 31). A shard sends either none or exactly 2 pairs to a group; a group receives at most 24 pairs in all, and some group exactly 24.
All inputs are finite; a program needn't handle non-finite values.
Results may differ from the reference program's by a relative error of at most 0.0045.
The reference program's roundings to bfloat16 on the way (of `normed`, `attn_weights` and `context`) count: a program that leaves them out, or rounds other values in their place, can miss the bound.
Values may be sent and summed in bfloat16 or wider, within the bound.
No kernel may reach another device: no remote copies, remote signals or barrier semaphores. Data moves between devices by JAX's collectives and lax.ppermute only.
A program may use at most 128 MiB of HBM per device.

```python
import math
import jax
import jax.numpy as jnp
from jax import lax

D = 2048
HD = 128
L = 128
CAP = 2
CAND = 16
BANK = 16
GCAP = 24
N_DP = 32


def draw_candidates(key, part):
    key = jax.random.fold_in(key, 11)
    key_perm, key_shuffle, key_source, key_target = jax.random.split(key, 4)
    half_groups = N_DP // 2
    groups_each = CAND // CAP
    hot_groups = min(3 * groups_each // 4, half_groups)
    group_perm = jax.random.permutation(key_perm, N_DP).astype(jnp.int32)
    shard_ids = jnp.arange(N_DP, dtype=jnp.int32)[:, None]
    offsets = jnp.arange(groups_each, dtype=jnp.int32)[None, :]
    residue = jnp.where(offsets < hot_groups, (shard_ids + offsets) % half_groups, half_groups + (shard_ids + offsets - hot_groups) % half_groups)
    chosen = jnp.take(group_perm, residue, axis=0)
    destination = jnp.repeat(chosen, CAP, axis=1)
    shuffles = jax.vmap(lambda sub_key: jax.random.permutation(sub_key, CAND))(jax.random.split(key_shuffle, N_DP))
    destination = jnp.take_along_axis(destination, shuffles.astype(jnp.int32), axis=1)
    source_ids = jax.random.randint(key_source, (N_DP, CAND), 0, BANK, dtype=jnp.int32)
    target_ids = jax.random.randint(key_target, (N_DP, CAND), 0, BANK, dtype=jnp.int32)
    stacked = jnp.stack([source_ids, target_ids, destination.astype(jnp.int32)], axis=-1)
    return stacked.reshape(N_DP * CAND, 3).astype(jnp.int32)


def draw_enc_bank(key, part):
    key = jax.random.fold_in(key, 5)
    key_base = jax.random.fold_in(key, 0)
    shape = (N_DP * BANK, L, D)
    states = jnp.clip(jax.random.normal(key_base, shape, jnp.float32), -6.0, 6.0)
    return states.astype(jnp.bfloat16)


def touch_ends(entries, rng, smallest, top_value):
    shape = entries.shape
    spot = [jax.random.randint(jax.random.fold_in(rng, axis), (), 0, shape[axis]) for axis in range(len(shape))]
    entries = entries.at[tuple(spot)].set(smallest)
    longest = shape.index(max(shape))
    spot[longest] = (spot[longest] + 1) % shape[longest]
    return entries.at[tuple(spot)].set(top_value)


def level_of(rng, extent, cuts, low, largest):
    loudness = 1.0
    for axis_at, parts in cuts:
        draws = jax.random.uniform(jax.random.fold_in(jax.random.fold_in(rng, 6), axis_at), (parts,), jnp.float32, low / len(cuts), largest / len(cuts))
        loudness = loudness * jnp.repeat(jnp.exp(draws), extent[axis_at] // parts).reshape((-1,) + (1,) * (len(extent) - 1 - axis_at))
    return loudness


def scatter_about(stream_key, shape, spread, most, shards=(), kind=jnp.bfloat16):
    factor_of = level_of(stream_key, shape, shards, -0.22, 0.18) if shards else 1.0
    drawn = jax.random.normal(stream_key, shape, jnp.float32) * spread * factor_of
    return jnp.minimum(jnp.maximum(drawn, -most), most).astype(kind)


def setup_inputs(seed: int = 0) -> dict:
    keys = jax.random.split(jax.random.key(seed), 8)
    return {
        "candidates": draw_candidates(jax.random.fold_in(keys[7], 71), 0),
        "row_lengths": touch_ends(jax.random.randint(keys[1], (N_DP * BANK, 2), 1, L + 1), jax.random.fold_in(keys[1], 1), 1, L).astype(jnp.int32),
        "enc_bank": draw_enc_bank(jax.random.fold_in(keys[7], 71), 0),
        "dec_bank": scatter_about(keys[3], (N_DP * BANK, L, D), 1.0, 6.0, ((0, 32), (2, 4))),
        "w_query": scatter_about(keys[4], (D, D), D ** -0.5, 0.125, ((1, 4),)),
        "w_key": scatter_about(keys[5], (D, D), D ** -0.5, 0.125, ((1, 4),)),
        "w_value": scatter_about(keys[6], (D, D), D ** -0.5, 0.125, ((1, 4),)),
    }


def attend(source_rows, target_rows, source_length, target_length, w_query, w_key, w_value):
    pair_count = target_rows.shape[0]
    local_width = w_query.shape[1]
    head_count = local_width // HD
    rows_f = target_rows.astype(jnp.float32)
    row_mean = lax.optimization_barrier(jnp.mean(rows_f, axis=-1, keepdims=True))
    centred = rows_f - row_mean
    variance = lax.optimization_barrier(jnp.mean(centred * centred, axis=-1, keepdims=True))
    normed = (centred * lax.rsqrt(variance + 1e-05)).astype(jnp.bfloat16)
    queries = jnp.dot(normed.reshape(-1, D), w_query, preferred_element_type=jnp.float32).astype(jnp.bfloat16)
    key_rows = jnp.dot(source_rows.reshape(-1, D), w_key, preferred_element_type=jnp.float32).astype(jnp.bfloat16)
    value_rows = jnp.dot(source_rows.reshape(-1, D), w_value, preferred_element_type=jnp.float32).astype(jnp.bfloat16)
    queries = queries.reshape(pair_count, L, head_count, HD).astype(jnp.float32)
    key_rows = key_rows.reshape(pair_count, L, head_count, HD).astype(jnp.float32)
    value_rows = value_rows.reshape(pair_count, L, head_count, HD).astype(jnp.float32)
    scores = jnp.einsum('plhd,pmhd->phlm', queries, key_rows, precision=lax.Precision.HIGHEST) * (1.0 / math.sqrt(HD))
    positions = jnp.arange(L, dtype=jnp.int32)
    key_mask = positions[None, None, None, :] < source_length[:, None, None, None]
    scores = jnp.where(key_mask, scores, -1e+30)
    biggest = lax.optimization_barrier(jnp.max(scores, axis=-1, keepdims=True))
    expo_terms = jnp.exp(scores - biggest)
    totals = lax.optimization_barrier(jnp.sum(expo_terms, axis=-1, keepdims=True))
    attn_weights = (expo_terms / totals).astype(jnp.bfloat16).astype(jnp.float32)
    context = jnp.einsum('phlm,pmhd->plhd', attn_weights, value_rows, precision=lax.Precision.HIGHEST)
    query_mask = positions[None, :, None, None] < target_length[:, None, None, None]
    context = jnp.where(query_mask, context, 0.0).astype(jnp.bfloat16)
    return context.reshape(pair_count, L, local_width)

def reference(candidates, row_lengths, enc_bank, dec_bank, w_query, w_key, w_value):
    total_pairs = N_DP * CAND
    flat_index = jnp.arange(total_pairs, dtype=jnp.int32)
    bank_base = flat_index // CAND * BANK
    source_ids = bank_base + candidates[:, 0]
    target_ids = bank_base + candidates[:, 1]
    destination = candidates[:, 2]
    source_length = jnp.take(row_lengths[:, 0], source_ids, axis=0)
    target_length = jnp.take(row_lengths[:, 1], target_ids, axis=0)

    def one_shard(shard_index):
        start = (shard_index * CAND).astype(jnp.int32)
        src_part = lax.dynamic_slice_in_dim(source_ids, start, CAND)
        tgt_part = lax.dynamic_slice_in_dim(target_ids, start, CAND)
        src_len = lax.dynamic_slice_in_dim(source_length, start, CAND)
        tgt_len = lax.dynamic_slice_in_dim(target_length, start, CAND)
        source_rows = jnp.take(enc_bank, src_part, axis=0)
        target_rows = jnp.take(dec_bank, tgt_part, axis=0)
        return attend(source_rows, target_rows, src_len, tgt_len, w_query, w_key, w_value)
    context = lax.map(one_shard, jnp.arange(N_DP, dtype=jnp.int32)).reshape(total_pairs, L, D)
    onehot = (destination[:, None] == jnp.arange(N_DP, dtype=jnp.int32)[None, :]).astype(jnp.int32)
    earlier = jnp.cumsum(onehot, axis=0) - onehot
    rank_in = lax.optimization_barrier(jnp.sum(earlier * onehot, axis=1)).astype(jnp.int32)
    slot = (destination * GCAP + rank_in).astype(jnp.int32)
    contexts = jnp.zeros((N_DP * GCAP, L, D), jnp.bfloat16).at[slot].set(context)
    return contexts
```

```python
import functools
import math

import jax
import jax.numpy as jnp
from jax import lax
from jax.experimental import pallas as pl
from jax.experimental.pallas import tpu as pltpu
from jax.sharding import PartitionSpec as P

D = 2048
HD = 128
L = 128
GCAP = 24
BLOCK = 16
BLOCKS = L // BLOCK
TILE = 256
SIZES = (768, 1024, 1152, 1280, 1408, 1536, 1664, 1792, 1920, 2048, 2304, 2560, 3072, 4096)
VMEM = pl.BlockSpec(memory_space=pltpu.VMEM)
SMEM = pl.BlockSpec(memory_space=pltpu.SMEM)


def pack_kernel(table, enc, dec, out):
    size = out.shape[0] // BLOCK
    for bank, column in ((enc, 0), (dec, 2)):
        for row in range(bank.shape[0] // L):
            first = table[column + 1, row]

            def move(b, carry, bank=bank, row=row, first=first):
                to = pl.multiple_of((first + b) * BLOCK, BLOCK)
                out[pl.ds(to, BLOCK), :] = bank[pl.ds(pl.multiple_of(row * L + b * BLOCK, BLOCK), BLOCK), :]
                return carry

            lax.fori_loop(0, table[column, row], move, 0)
    used = table[4, 0] + table[4, 1]

    def clear(b, carry):
        out[pl.ds(pl.multiple_of(b * BLOCK, BLOCK), BLOCK), :] = jnp.zeros((BLOCK, out.shape[1]), out.dtype)
        return carry

    lax.fori_loop(used, size, clear, 0)


def attend_kernel(table, pairs, x0, x1, x2, x3, wq, wk, wv, out, keys, values, queries):
    rows, width = x0.shape
    heads = width // HD
    parts = (x0, x1, x2, x3)
    me = table[4, 2]
    starts = [pl.multiple_of(lax.rem(me + (4 - d), 4) * width, width) for d in range(4)]
    source = table[4, 0] * BLOCK
    target = table[4, 1] * BLOCK

    def kv_tile(i, carry):
        at = pl.multiple_of(jnp.minimum(i * TILE, rows - TILE), BLOCK)
        key_sum = jnp.zeros((TILE, width), jnp.float32)
        value_sum = jnp.zeros((TILE, width), jnp.float32)
        for part, start in zip(parts, starts):
            x = part[pl.ds(at, TILE), :]
            key_sum += jnp.dot(x, wk[pl.ds(start, width), :], preferred_element_type=jnp.float32)
            value_sum += jnp.dot(x, wv[pl.ds(start, width), :], preferred_element_type=jnp.float32)
        keys[pl.ds(at, TILE), :] = key_sum.astype(jnp.bfloat16)
        values[pl.ds(at, TILE), :] = value_sum.astype(jnp.bfloat16)
        return carry

    tiles = (source + TILE - 1) // TILE
    lax.fori_loop(0, tiles, kv_tile, 0)
    after = pl.multiple_of(jnp.minimum(tiles * TILE, rows), BLOCK)
    values[pl.ds(after, L), :] = jnp.zeros((L, width), jnp.bfloat16)

    def q_tile(i, carry):
        at = pl.multiple_of(jnp.minimum(source + i * TILE, rows - TILE), BLOCK)
        xs = [part[pl.ds(at, TILE), :].astype(jnp.float32) for part in parts]
        mean = sum(jnp.sum(x, axis=-1, keepdims=True) for x in xs) * (1.0 / D)
        xs = [x - mean for x in xs]
        variance = sum(jnp.sum(x * x, axis=-1, keepdims=True) for x in xs) * (1.0 / D)
        scale = lax.rsqrt(variance + 1e-05)
        total = jnp.zeros((TILE, width), jnp.float32)
        for x, start in zip(xs, starts):
            total += jnp.dot(
                (x * scale).astype(jnp.bfloat16), wq[pl.ds(start, width), :], preferred_element_type=jnp.float32
            )
        queries[pl.ds(at, TILE), :] = total.astype(jnp.bfloat16)
        return carry

    lax.fori_loop(0, (target + TILE - 1) // TILE, q_tile, 0)
    column = lax.broadcasted_iota(jnp.int32, (L, L), 1)
    line = lax.broadcasted_iota(jnp.int32, (L, HD), 0)

    def pair(p, carry):
        s_at = pl.multiple_of(pairs[0, p], BLOCK)
        t_at = pl.multiple_of(pairs[1, p], BLOCK)
        to = pl.multiple_of(p * 32, 32)
        key_mask = column < pairs[2, p]
        query_mask = line < pairs[3, p]
        for h in range(heads):
            cols = slice(h * HD, (h + 1) * HD)
            scores = lax.dot_general(
                queries[pl.ds(t_at, L), cols],
                keys[pl.ds(s_at, L), cols],
                (((1,), (1,)), ((), ())),
                preferred_element_type=jnp.float32,
            ) * (1.0 / math.sqrt(HD))
            scores = jnp.where(key_mask, scores, -1e30)
            terms = jnp.exp(scores - jnp.max(scores, axis=-1, keepdims=True))
            weights = (terms / jnp.sum(terms, axis=-1, keepdims=True)).astype(jnp.bfloat16)
            context = jnp.dot(weights, values[pl.ds(s_at, L), cols], preferred_element_type=jnp.float32)
            context = jnp.where(query_mask, context, 0.0).astype(jnp.bfloat16)
            for g in range(4):
                out[pl.ds(to, 32), g * width + h * HD : g * width + (h + 1) * HD] = context[g * 32 : (g + 1) * 32]
        return carry

    lax.fori_loop(0, out.shape[0] // 32, pair, 0)


def place_kernel(x, out):
    slots = out.shape[0]
    rows = x.shape[0]
    width = out.shape[2]
    first = pl.program_id(0) * slots
    line = lax.broadcasted_iota(jnp.int32, (slots * 32, rows), 0)
    column = lax.broadcasted_iota(jnp.int32, (slots * 32, rows), 1)
    wanted = (line % 32) * GCAP + first + line // 32
    pick = jnp.where(column == wanted, 1.0, 0.0).astype(jnp.bfloat16)
    moved = jnp.dot(pick, x[...], preferred_element_type=jnp.float32).astype(jnp.bfloat16)
    for s in range(slots):
        for g in range(4):
            out[s, g * 32 : (g + 1) * 32, :] = moved[s * 32 : (s + 1) * 32, g * width : (g + 1) * width]


def earlier(counts):
    ids = jnp.arange(counts.shape[0], dtype=jnp.int32)
    return jnp.sum(jnp.where(ids[None, :] < ids[:, None], counts[None, :], 0), axis=1)


def pick(values, ids):
    rows = jnp.arange(values.shape[0], dtype=jnp.int32)
    return jnp.sum(jnp.where(ids[:, None] == rows[None, :], values[None, :], 0), axis=1)


def gather_and_attend(size, table, pairs, enc, dec, wq, wk, wv):
    width = enc.shape[1]
    own = pl.pallas_call(
        pack_kernel,
        out_shape=jax.ShapeDtypeStruct((size, width), jnp.bfloat16),
        in_specs=[SMEM, VMEM, VMEM],
        out_specs=VMEM,
        compiler_params=pltpu.CompilerParams(vmem_limit_bytes=40 * 2**20),
    )(table, enc, dec)
    ring = lambda step: [(i, (i + step) % 4) for i in range(4)]
    send = lambda x, step: lax.ppermute(x, "mp", ring(step))
    half, quarter = size // 2, size // 4
    left, right, across = [], [], []
    for c in range(2):
        part = own[c * half : (c + 1) * half]
        left.append(send(part, 1))
        right.append(send(part, 3))
    for c in range(2):
        across.append(send(left[c][:quarter], 1))
        across.append(send(right[c][quarter:], 3))
    x1, x3, x2 = jnp.concatenate(left), jnp.concatenate(right), jnp.concatenate(across)
    return pl.pallas_call(
        attend_kernel,
        out_shape=jax.ShapeDtypeStruct((pairs.shape[1] * 32, 4 * width), jnp.bfloat16),
        in_specs=[SMEM, SMEM] + [VMEM] * 7,
        out_specs=VMEM,
        scratch_shapes=[pltpu.VMEM((size + L, width), jnp.bfloat16)] * 3,
        compiler_params=pltpu.CompilerParams(vmem_limit_bytes=56 * 2**20),
    )(table, pairs, own, x1, x2, x3, wq, wk, wv)


def on_device(candidates, row_lengths, enc_bank, dec_bank, w_query, w_key, w_value):
    shards = lax.axis_size("dp")
    count = candidates.shape[0]
    bank = enc_bank.shape[0]
    width = enc_bank.shape[2]
    source_ids, target_ids, destination = candidates[:, 0], candidates[:, 1], candidates[:, 2]
    ids = jnp.arange(bank, dtype=jnp.int32)
    spans = []
    for column, chosen in ((0, source_ids), (1, target_ids)):
        needed = jnp.any(chosen[None, :] == ids[:, None], axis=1)
        spans.append(jnp.where(needed, (row_lengths[:, column] + BLOCK - 1) // BLOCK, 0))
    totals = [jnp.sum(s) for s in spans]
    source_at = earlier(spans[0])
    target_at = earlier(spans[1]) + totals[0]
    head = jnp.zeros((bank,), jnp.int32)
    last = jnp.where(ids == 0, totals[0], jnp.where(ids == 1, totals[1], lax.axis_index("mp")))
    table = jnp.stack([spans[0], source_at, spans[1], target_at, last, head, head, head])
    pairs = jnp.stack(
        [
            pick(source_at, source_ids) * BLOCK,
            pick(target_at, target_ids) * BLOCK,
            pick(row_lengths[:, 0], source_ids),
            pick(row_lengths[:, 1], target_ids),
        ]
    )
    needed = (totals[0] + totals[1]) * BLOCK
    bucket = jnp.sum((needed > jnp.array(SIZES[:-1], jnp.int32)).astype(jnp.int32))
    all_dest = lax.all_gather(
        jnp.broadcast_to(destination.astype(jnp.bfloat16)[:, None], (count, 128)), "dp", axis=0, tiled=True
    )[:, 0].astype(jnp.int32)
    context = lax.switch(
        bucket,
        [functools.partial(gather_and_attend, size) for size in SIZES],
        table,
        pairs,
        enc_bank.reshape(bank * L, width),
        dec_bank.reshape(bank * L, width),
        w_query,
        w_key,
        w_value,
    )
    n = count * 32
    line = jnp.arange(n, dtype=jnp.int32)
    order = (line % count) * 32 + line // count
    turn = (order[:, None] == line[None, :]).astype(jnp.bfloat16)
    pieces = jnp.dot(turn, context, preferred_element_type=jnp.float32).astype(jnp.bfloat16)
    spread = lax.all_to_all(pieces.reshape(shards, count, 4 * width), "dp", 0, 0, tiled=True)
    total = shards * count
    cand = jnp.arange(total, dtype=jnp.int32)
    rank = jnp.sum(
        ((all_dest[:, None] == all_dest[None, :]) & (cand[None, :] < cand[:, None])).astype(jnp.int32), axis=1
    )
    slot = all_dest * GCAP + rank
    choose = (jnp.arange(shards * GCAP, dtype=jnp.int32)[:, None] == slot[None, :]).astype(jnp.bfloat16)
    routed = jnp.dot(choose, spread.reshape(total, 4 * width), preferred_element_type=jnp.float32).astype(jnp.bfloat16)
    arrived = lax.all_to_all(routed.reshape(shards, GCAP, 4 * width), "dp", 0, 0, tiled=True)
    return pl.pallas_call(
        place_kernel,
        grid=(GCAP // 4,),
        out_shape=jax.ShapeDtypeStruct((GCAP, L, width), jnp.bfloat16),
        in_specs=[pl.BlockSpec((shards * GCAP, 4 * width), lambda i: (0, 0))],
        out_specs=pl.BlockSpec((4, L, width), lambda i: (i, 0, 0)),
        compiler_params=pltpu.CompilerParams(vmem_limit_bytes=40 * 2**20),
    )(arrived.reshape(shards * GCAP, 4 * width))


def solution(mesh):
    placed = (
        P("dp", None),
        P("dp", None),
        P("dp", None, "mp"),
        P("dp", None, "mp"),
        P(None, "mp"),
        P(None, "mp"),
        P(None, "mp"),
    )
    return jax.shard_map(on_device, mesh=mesh, in_specs=placed, out_specs=P("dp", None, "mp"), check_vma=False)
```

```python
import functools
import math

import jax
import jax.numpy as jnp
from jax import lax
from jax.experimental import pallas as pl
from jax.experimental.pallas import tpu as pltpu
from jax.sharding import PartitionSpec as P

D = 2048
HD = 128
L = 128
GCAP = 24
BLOCK = 16
BLOCKS = L // BLOCK
TILE = 256
SIZES = (1024, 1280, 1408, 1536, 1664, 1792, 2048, 2560, 4096)
VMEM = pl.BlockSpec(memory_space=pltpu.VMEM)
SMEM = pl.BlockSpec(memory_space=pltpu.SMEM)


def pack_kernel(cand, lens, enc, dec, out_pairs, out_bucket, out, out_table):
    rows = enc.shape[0] // L
    count = cand.shape[0]
    for row in range(rows):
        out_table[0, row] = 0
        out_table[1, row] = 0

    def mark(c, carry):
        out_table[0, cand[c, 0]] = 1
        out_table[1, cand[c, 1]] = 1
        return carry

    lax.fori_loop(0, count, mark, 0)
    at = jnp.int32(0)
    ends = []
    for column, bank in ((0, enc), (1, dec)):
        for row in range(rows):
            blocks = jnp.where(out_table[column, row] > 0, (lens[row, column] + BLOCK - 1) // BLOCK, 0)
            out_table[column, row] = at * BLOCK

            def move(b, carry, bank=bank, row=row, first=at):
                to = pl.multiple_of((first + b) * BLOCK, BLOCK)
                out[pl.ds(to, BLOCK), :] = bank[pl.ds(pl.multiple_of(row * L + b * BLOCK, BLOCK), BLOCK), :]
                return carry

            lax.fori_loop(0, blocks, move, 0)
            at = at + blocks
        ends.append(at)
    bucket = jnp.int32(0)
    size = jnp.int32(SIZES[0])
    for low, high in zip(SIZES, SIZES[1:]):
        over = at * BLOCK > low
        bucket = bucket + over.astype(jnp.int32)
        size = jnp.where(over, high, size)
    out_bucket[0] = bucket
    out_bucket[1] = ends[0] * BLOCK
    out_bucket[2] = (ends[1] - ends[0]) * BLOCK

    def place(c, carry):
        s, t = cand[c, 0], cand[c, 1]
        out_pairs[0, c] = out_table[0, s]
        out_pairs[1, c] = out_table[1, t]
        out_pairs[2, c] = lens[s, 0]
        out_pairs[3, c] = lens[t, 1]
        out_pairs[4, c] = cand[c, 2]
        return carry

    lax.fori_loop(0, count, place, 0)

    def clear(b, carry):
        out[pl.ds(pl.multiple_of(b * BLOCK, BLOCK), BLOCK), :] = jnp.zeros((BLOCK, out.shape[1]), out.dtype)
        return carry

    lax.fori_loop(at, size // BLOCK, clear, 0)


def attend_kernel(facts, pairs, x0, x1, x2, x3, wq, wk, wv, out, keys, values, queries, turned):
    rows, width = x0.shape
    heads = width // HD
    parts = (x0, x1, x2, x3)
    me = lax.axis_index("mp")
    starts = [pl.multiple_of(lax.rem(me + (4 - d), 4) * width, width) for d in range(4)]
    source = pl.multiple_of(facts[1], BLOCK)
    target = facts[2]
    count = pairs.shape[1]

    def kv_tile(i, carry):
        at = pl.multiple_of(jnp.minimum(i * TILE, rows - TILE), BLOCK)
        key_sum = jnp.zeros((TILE, width), jnp.float32)
        value_sum = jnp.zeros((TILE, width), jnp.float32)
        for part, start in zip(parts, starts):
            x = part[pl.ds(at, TILE), :]
            key_sum += jnp.dot(x, wk[pl.ds(start, width), :], preferred_element_type=jnp.float32)
            value_sum += jnp.dot(x, wv[pl.ds(start, width), :], preferred_element_type=jnp.float32)
        keys[pl.ds(at, TILE), :] = key_sum.astype(jnp.bfloat16)
        values[pl.ds(at, TILE), :] = value_sum.astype(jnp.bfloat16)
        return carry

    tiles = (source + TILE - 1) // TILE
    lax.fori_loop(0, tiles, kv_tile, 0)
    after = pl.multiple_of(jnp.minimum(tiles * TILE, rows), BLOCK)
    values[pl.ds(after, L), :] = jnp.zeros((L, width), jnp.bfloat16)

    def q_tile(i, carry):
        at = pl.multiple_of(jnp.minimum(source + i * TILE, rows - TILE), BLOCK)
        xs = [part[pl.ds(at, TILE), :].astype(jnp.float32) for part in parts]
        mean = sum(jnp.sum(x, axis=-1, keepdims=True) for x in xs) * (1.0 / D)
        xs = [x - mean for x in xs]
        variance = sum(jnp.sum(x * x, axis=-1, keepdims=True) for x in xs) * (1.0 / D)
        scale = lax.rsqrt(variance + 1e-05)
        total = jnp.zeros((TILE, width), jnp.float32)
        for x, start in zip(xs, starts):
            total += jnp.dot(
                (x * scale).astype(jnp.bfloat16), wq[pl.ds(start, width), :], preferred_element_type=jnp.float32
            )
        queries[pl.ds(at, TILE), :] = total.astype(jnp.bfloat16)
        return carry

    lax.fori_loop(0, (target + TILE - 1) // TILE, q_tile, 0)
    column = lax.broadcasted_iota(jnp.int32, (L, L), 1)
    line = lax.broadcasted_iota(jnp.int32, (L, HD), 0)

    def pair(p, carry):
        s_at = pl.multiple_of(pairs[0, p], BLOCK)
        t_at = pl.multiple_of(pairs[1, p], BLOCK)
        key_mask = column < pairs[2, p]
        query_mask = line < pairs[3, p]
        cols = [slice(h * HD, (h + 1) * HD) for h in range(heads)]
        scores = [
            lax.dot_general(
                queries[pl.ds(t_at, L), c],
                keys[pl.ds(s_at, L), c],
                (((1,), (1,)), ((), ())),
                preferred_element_type=jnp.float32,
            )
            for c in cols
        ]
        scores = [jnp.where(key_mask, s * (1.0 / math.sqrt(HD)), -1e30) for s in scores]
        tops = [jnp.max(s, axis=-1, keepdims=True) for s in scores]
        terms = [jnp.exp(s - top) for s, top in zip(scores, tops)]
        sums = [jnp.sum(t, axis=-1, keepdims=True) for t in terms]
        weights = [(t * (1.0 / total)).astype(jnp.bfloat16) for t, total in zip(terms, sums)]
        contexts = [
            jnp.dot(w, values[pl.ds(s_at, L), c], preferred_element_type=jnp.float32)
            for w, c in zip(weights, cols)
        ]
        for h, context in enumerate(contexts):
            context = jnp.where(query_mask, context, 0.0)
            for g in range(4):
                turned[h + g * heads, pl.ds(p, 32, stride=count), :] = context[g * 32 : (g + 1) * 32]
        return carry

    lax.fori_loop(0, count, pair, 0)
    for k in range(4 * heads):
        g, h = k // heads, k % heads
        at = g * width + h * HD
        out[:, at : at + HD] = turned[k].astype(jnp.bfloat16)
    line = lax.broadcasted_iota(jnp.int32, (count, HD), 0)
    groups = jnp.zeros((count, HD), jnp.float32)
    for p in range(count):
        groups = jnp.where(line == p, pairs[4, p].astype(jnp.float32), groups)
    for j in range(32):
        out[j * count : (j + 1) * count, 4 * width :] = groups.astype(jnp.bfloat16)


def route_kernel(x, out):
    total = x.shape[0]
    width = out.shape[1]
    mine = x[:, width : width + 1].astype(jnp.float32)
    a = lax.broadcasted_iota(jnp.int32, (total, total), 0)
    b = lax.broadcasted_iota(jnp.int32, (total, total), 1)
    ones = jnp.ones((16, total), jnp.bfloat16)
    spread = jnp.where(a == b, mine, 0.0).astype(jnp.bfloat16)
    group = jnp.dot(ones, spread, preferred_element_type=jnp.float32)[:1]
    before = jnp.where((mine == group) & (a < b), 1.0, 0.0).astype(jnp.bfloat16)
    rank = jnp.dot(ones, before, preferred_element_type=jnp.float32)[:1]
    slot = (group * GCAP + rank).astype(jnp.int32)
    choose = lax.broadcasted_iota(jnp.int32, (out.shape[0], total), 0) == slot
    choose = jnp.where(choose, 1.0, 0.0).astype(jnp.bfloat16)
    for c in range(0, width, 256):
        out[:, c : c + 256] = jnp.dot(choose, x[:, c : c + 256], preferred_element_type=jnp.float32).astype(
            jnp.bfloat16
        )


def place_kernel(x, out):
    slots = out.shape[0]
    rows = x.shape[0]
    width = out.shape[2]
    first = pl.program_id(0) * slots
    line = lax.broadcasted_iota(jnp.int32, (slots * 32, rows), 0)
    column = lax.broadcasted_iota(jnp.int32, (slots * 32, rows), 1)
    wanted = (line % 32) * GCAP + first + line // 32
    pick = jnp.where(column == wanted, 1.0, 0.0).astype(jnp.bfloat16)
    moved = jnp.dot(pick, x[...], preferred_element_type=jnp.float32).astype(jnp.bfloat16)
    for s in range(slots):
        for g in range(4):
            out[s, g * 32 : (g + 1) * 32, :] = moved[s * 32 : (s + 1) * 32, g * width : (g + 1) * width]


def gather_and_attend(size, facts, pairs, packed, wq, wk, wv):
    width = packed.shape[1]
    own = packed[:size]
    ring = lambda step: [(i, (i + step) % 4) for i in range(4)]
    send = lambda x, step: lax.ppermute(x, "mp", ring(step))
    half, quarter = size // 2, size // 4
    left, right, across = [], [], []
    for c in range(2):
        part = own[c * half : (c + 1) * half]
        left.append(send(part, 1))
        right.append(send(part, 3))
    for c in range(2):
        across.append(send(left[c][:quarter], 1))
        across.append(send(right[c][quarter:], 3))
    x1, x3, x2 = jnp.concatenate(left), jnp.concatenate(right), jnp.concatenate(across)
    n = pairs.shape[1] * 32
    return pl.pallas_call(
        attend_kernel,
        out_shape=jax.ShapeDtypeStruct((n, 4 * width + HD), jnp.bfloat16),
        in_specs=[SMEM, SMEM] + [VMEM] * 7,
        out_specs=VMEM,
        scratch_shapes=[pltpu.VMEM((size + L, width), jnp.bfloat16)] * 3
        + [pltpu.VMEM((4 * width // HD, n, HD), jnp.float32)],
        compiler_params=pltpu.CompilerParams(vmem_limit_bytes=60 * 2**20),
    )(facts, pairs, own, x1, x2, x3, wq, wk, wv)


def on_device(candidates, row_lengths, enc_bank, dec_bank, w_query, w_key, w_value):
    shards = lax.axis_size("dp")
    count = candidates.shape[0]
    bank = enc_bank.shape[0]
    width = enc_bank.shape[2]
    pairs, facts, packed = pl.pallas_call(
        pack_kernel,
        out_shape=[
            jax.ShapeDtypeStruct((5, count), jnp.int32),
            jax.ShapeDtypeStruct((4,), jnp.int32),
            jax.ShapeDtypeStruct((2 * bank * L, width), jnp.bfloat16),
        ],
        in_specs=[SMEM, SMEM, VMEM, VMEM],
        out_specs=[SMEM, SMEM, VMEM],
        scratch_shapes=[pltpu.SMEM((2, bank), jnp.int32)],
        compiler_params=pltpu.CompilerParams(vmem_limit_bytes=40 * 2**20),
    )(candidates, row_lengths, enc_bank.reshape(bank * L, width), dec_bank.reshape(bank * L, width))
    context = lax.switch(
        facts[0],
        [functools.partial(gather_and_attend, size) for size in SIZES],
        facts,
        pairs,
        packed,
        w_query,
        w_key,
        w_value,
    )
    spread = lax.all_to_all(context.reshape(shards, count, 4 * width + HD), "dp", 0, 0, tiled=True)
    routed = pl.pallas_call(
        route_kernel,
        out_shape=jax.ShapeDtypeStruct((shards * GCAP, 4 * width), jnp.bfloat16),
        in_specs=[VMEM],
        out_specs=VMEM,
        compiler_params=pltpu.CompilerParams(vmem_limit_bytes=40 * 2**20),
    )(spread.reshape(shards * count, 4 * width + HD))
    arrived = lax.all_to_all(routed.reshape(shards, GCAP, 4 * width), "dp", 0, 0, tiled=True)
    return pl.pallas_call(
        place_kernel,
        grid=(GCAP // 4,),
        out_shape=jax.ShapeDtypeStruct((GCAP, L, width), jnp.bfloat16),
        in_specs=[pl.BlockSpec((shards * GCAP, 4 * width), lambda i: (0, 0))],
        out_specs=pl.BlockSpec((4, L, width), lambda i: (i, 0, 0)),
        compiler_params=pltpu.CompilerParams(vmem_limit_bytes=40 * 2**20),
    )(arrived.reshape(shards * GCAP, 4 * width))


def solution(mesh):
    placed = (
        P("dp", None),
        P("dp", None),
        P("dp", None, "mp"),
        P("dp", None, "mp"),
        P(None, "mp"),
        P(None, "mp"),
        P(None, "mp"),
    )
    return jax.shard_map(on_device, mesh=mesh, in_specs=placed, out_specs=P("dp", None, "mp"), check_vma=False)
```

```python
import functools
import math

import jax
import jax.numpy as jnp
from jax import lax
from jax.experimental import pallas as pl
from jax.experimental.pallas import tpu as pltpu
from jax.sharding import PartitionSpec as P

D = 2048
HD = 128
L = 128
GCAP = 24
BLOCK = 16
BLOCKS = L // BLOCK
TILE = 256
SIZES = (1408, 1536, 1664, 1792, 1920, 2048, 2304, 4096)
VMEM = pl.BlockSpec(memory_space=pltpu.VMEM)
SMEM = pl.BlockSpec(memory_space=pltpu.SMEM)
HBM = pl.BlockSpec(memory_space=pltpu.HBM)


def pack_kernel(cand, lens, enc, dec, out_pairs, facts, out, staged, starts, arrived):
    rows = enc.shape[0] // L
    count = cand.shape[1]
    for row in range(rows):
        starts[0, row] = 0
        starts[1, row] = 0
    for c in range(count):
        starts[0, cand[0, c]] = 1
        starts[1, cand[1, c]] = 1
    banks = (enc, dec)

    def load(column, row):
        at = slice(row * L, (row + 1) * L)
        return pltpu.make_async_copy(banks[column].at[at], staged.at[column, at], arrived.at[column, row])

    for column in range(2):
        for row in range(rows):

            @pl.when(starts[column, row] > 0)
            def _(column=column, row=row):
                load(column, row).start()

    total = jnp.int32(0)
    for column in range(2):
        for row in range(rows):
            needed = starts[column, row] > 0
            blocks = jnp.where(needed, (lens[column, row] + BLOCK - 1) // BLOCK, 0)
            starts[column, row] = total * BLOCK

            @pl.when(needed)
            def _(column=column, row=row):
                load(column, row).wait()

            def move(b, carry, column=column, row=row, first=total):
                to = pl.multiple_of((first + b) * BLOCK, BLOCK)
                out[pl.ds(to, BLOCK), :] = staged[column, pl.ds(pl.multiple_of(row * L + b * BLOCK, BLOCK), BLOCK), :]
                return carry

            lax.fori_loop(0, blocks, move, 0)
            total = total + blocks
        facts[1 + column] = total * BLOCK
    bucket = jnp.int32(0)
    size = jnp.int32(SIZES[0])
    for low, high in zip(SIZES, SIZES[1:]):
        over = total * BLOCK > low
        bucket = bucket + over.astype(jnp.int32)
        size = jnp.where(over, high, size)
    facts[0] = bucket

    def place(c, carry):
        s, t = cand[0, c], cand[1, c]
        out_pairs[0, c] = starts[0, s]
        out_pairs[1, c] = starts[1, t]
        out_pairs[2, c] = lens[0, s]
        out_pairs[3, c] = lens[1, t]
        out_pairs[4, c] = cand[2, c]
        return carry

    lax.fori_loop(0, count, place, 0)

    def clear(b, carry):
        out[pl.ds(pl.multiple_of(b * BLOCK, BLOCK), BLOCK), :] = jnp.zeros((BLOCK, out.shape[1]), out.dtype)
        return carry

    lax.fori_loop(total, size // BLOCK, clear, 0)


def assemble_kernel(*refs):
    pieces, (out1, out2, out3, done) = refs[:8], refs[8:]
    half = pieces[0].shape[0]
    quarter = half // 2
    outs = (out1.at[:half], out3.at[:half], out1.at[half : 2 * half], out3.at[half : 2 * half]) + tuple(
        out2.at[k * quarter : (k + 1) * quarter] for k in range(4)
    )
    copies = [pltpu.make_async_copy(piece, out, done.at[k]) for k, (piece, out) in enumerate(zip(pieces, outs))]
    for copy in copies:
        copy.start()
    for copy in copies:
        copy.wait()


def attend_kernel(facts, pairs, x0, x1, x2, x3, wq, wk, wv, out, xs, keys, values, queries, turned, arrived):
    width = x0.shape[1]
    heads = width // HD
    me = lax.axis_index("mp")
    origin = [pl.multiple_of(lax.rem(me + (4 - d), 4) * width, width) for d in range(4)]
    source = pl.multiple_of(facts[1], BLOCK)
    target = facts[2] - facts[1]
    count = pairs.shape[1]
    chunks = (facts[2] + TILE - 1) // TILE
    tiles = (source + TILE - 1) // TILE

    def loads(i):
        rows = pl.ds(pl.multiple_of(i * TILE, TILE), TILE)
        return [
            pltpu.make_async_copy(x.at[rows], xs.at[d, rows], arrived.at[d, i]) for d, x in enumerate((x0, x1, x2, x3))
        ]

    def begin(i, carry):
        for copy in loads(i):
            copy.start()
        return carry

    def finish(i, carry):
        for copy in loads(i):
            copy.wait()
        return carry

    lax.fori_loop(0, chunks, begin, 0)

    def kv_tile(i, carry):
        finish(i, 0)
        rows = pl.ds(pl.multiple_of(i * TILE, TILE), TILE)
        key_sum = jnp.zeros((TILE, width), jnp.float32)
        value_sum = jnp.zeros((TILE, width), jnp.float32)
        for d in range(4):
            x = xs[d, rows, :]
            key_sum += jnp.dot(x, wk[pl.ds(origin[d], width), :], preferred_element_type=jnp.float32)
            value_sum += jnp.dot(x, wv[pl.ds(origin[d], width), :], preferred_element_type=jnp.float32)
        keys[rows, :] = key_sum.astype(jnp.bfloat16)
        values[rows, :] = value_sum.astype(jnp.bfloat16)
        return carry

    lax.fori_loop(0, tiles, kv_tile, 0)
    values[pl.ds(source, L), :] = jnp.zeros((L, width), jnp.bfloat16)
    lax.fori_loop(tiles, chunks, finish, 0)

    def q_tile(i, carry):
        rows = pl.ds(pl.multiple_of(source + i * TILE, BLOCK), TILE)
        parts = [xs[d, rows, :].astype(jnp.float32) for d in range(4)]
        mean = sum(jnp.sum(x, axis=-1, keepdims=True) for x in parts) * (1.0 / D)
        parts = [x - mean for x in parts]
        variance = sum(jnp.sum(x * x, axis=-1, keepdims=True) for x in parts) * (1.0 / D)
        scale = lax.rsqrt(variance + 1e-05)
        total = jnp.zeros((TILE, width), jnp.float32)
        for x, start in zip(parts, origin):
            total += jnp.dot(
                (x * scale).astype(jnp.bfloat16), wq[pl.ds(start, width), :], preferred_element_type=jnp.float32
            )
        queries[pl.ds(pl.multiple_of(i * TILE, TILE), TILE), :] = total.astype(jnp.bfloat16)
        return carry

    lax.fori_loop(0, (target + TILE - 1) // TILE, q_tile, 0)
    column = lax.broadcasted_iota(jnp.int32, (L, L), 1)
    line = lax.broadcasted_iota(jnp.int32, (L, HD), 0)

    def pair(p, carry):
        s_at = pl.multiple_of(pairs[0, p], BLOCK)
        t_at = pl.multiple_of(pairs[1, p] - source, BLOCK)
        key_mask = column < pairs[2, p]
        query_mask = line < pairs[3, p]
        cols = [slice(h * HD, (h + 1) * HD) for h in range(heads)]
        scores = [
            lax.dot_general(
                queries[pl.ds(t_at, L), c],
                keys[pl.ds(s_at, L), c],
                (((1,), (1,)), ((), ())),
                preferred_element_type=jnp.float32,
            )
            for c in cols
        ]
        scores = [jnp.where(key_mask, s * (1.0 / math.sqrt(HD)), -1e30) for s in scores]
        tops = [jnp.max(s, axis=-1, keepdims=True) for s in scores]
        terms = [jnp.exp(s - top) for s, top in zip(scores, tops)]
        sums = [jnp.sum(t, axis=-1, keepdims=True) for t in terms]
        weights = [(t * (1.0 / total)).astype(jnp.bfloat16) for t, total in zip(terms, sums)]
        contexts = [
            jnp.dot(w, values[pl.ds(s_at, L), c], preferred_element_type=jnp.float32)
            for w, c in zip(weights, cols)
        ]
        for h, context in enumerate(contexts):
            context = jnp.where(query_mask, context, 0.0)
            for g in range(4):
                turned[h + g * heads, pl.ds(p, 32, stride=count), :] = context[g * 32 : (g + 1) * 32]
        return carry

    lax.fori_loop(0, count, pair, 0)
    for k in range(4 * heads):
        g, h = k // heads, k % heads
        at = g * width + h * HD
        out[:, at : at + HD] = turned[k].astype(jnp.bfloat16)
    line = lax.broadcasted_iota(jnp.int32, (count, HD), 0)
    groups = jnp.zeros((count, HD), jnp.float32)
    for p in range(count):
        groups = jnp.where(line == p, pairs[4, p].astype(jnp.float32), groups)
    for j in range(32):
        out[j * count : (j + 1) * count, 4 * width :] = groups.astype(jnp.bfloat16)


def route_kernel(x, out):
    total = x.shape[0]
    width = out.shape[1]
    mine = x[:, width : width + 1].astype(jnp.float32)
    a = lax.broadcasted_iota(jnp.int32, (total, total), 0)
    b = lax.broadcasted_iota(jnp.int32, (total, total), 1)
    ones = jnp.ones((16, total), jnp.bfloat16)
    spread = jnp.where(a == b, mine, 0.0).astype(jnp.bfloat16)
    group = jnp.dot(ones, spread, preferred_element_type=jnp.float32)[:1]
    before = jnp.where((mine == group) & (a < b), 1.0, 0.0).astype(jnp.bfloat16)
    rank = jnp.dot(ones, before, preferred_element_type=jnp.float32)[:1]
    slot = (group * GCAP + rank).astype(jnp.int32)
    choose = lax.broadcasted_iota(jnp.int32, (out.shape[0], total), 0) == slot
    choose = jnp.where(choose, 1.0, 0.0).astype(jnp.bfloat16)
    for c in range(0, width, 256):
        out[:, c : c + 256] = jnp.dot(choose, x[:, c : c + 256], preferred_element_type=jnp.float32).astype(
            jnp.bfloat16
        )


def place_kernel(x, out, wide):
    slots, pieces, width = out.shape
    for c in range(width // HD):
        cols = slice(c * HD, (c + 1) * HD)
        wide[c] = x[:, cols].astype(jnp.float32)
    for q in range(slots):
        for c in range(width // HD):
            out[q, :, c * HD : (c + 1) * HD] = wide[c, pl.ds(q, pieces, stride=slots), :].astype(jnp.bfloat16)


def gather(size, packed):
    half, quarter = size // 2, size // 4
    send = lambda x, step: lax.ppermute(x, "mp", [(i, (i + step) % 4) for i in range(4)])
    direct, across = [], []
    for c in range(2):
        own = packed[c * half : (c + 1) * half]
        direct += [send(own, 1), send(own, 3)]
    for c in range(2):
        across += [send(direct[2 * c][:quarter], 1), send(direct[2 * c + 1][quarter:], 3)]
    return pl.pallas_call(
        assemble_kernel,
        out_shape=[jax.ShapeDtypeStruct(packed.shape, jnp.bfloat16)] * 3,
        in_specs=[VMEM] * 8,
        out_specs=[HBM] * 3,
        scratch_shapes=[pltpu.SemaphoreType.DMA((8,))],
        compiler_params=pltpu.CompilerParams(vmem_limit_bytes=13 * 2**20),
    )(*direct, *across)


def attend(facts, pairs, x0, x1, x2, x3, wq, wk, wv):
    total, width = x0.shape
    rows = total // 2
    n = pairs.shape[1] * 32
    return pl.pallas_call(
        attend_kernel,
        out_shape=jax.ShapeDtypeStruct((n, 4 * width + HD), jnp.bfloat16),
        in_specs=[SMEM, SMEM, VMEM] + [HBM] * 3 + [VMEM] * 3,
        out_specs=VMEM,
        scratch_shapes=[
            pltpu.VMEM((4, total + TILE, width), jnp.bfloat16),
            pltpu.VMEM((rows + L, width), jnp.bfloat16),
            pltpu.VMEM((rows + L, width), jnp.bfloat16),
            pltpu.VMEM((rows + L, width), jnp.bfloat16),
            pltpu.VMEM((4 * width // HD, n, HD), jnp.float32),
            pltpu.SemaphoreType.DMA((4, total // TILE)),
        ],
        compiler_params=pltpu.CompilerParams(vmem_limit_bytes=50 * 2**20),
    )(facts, pairs, x0, x1, x2, x3, wq, wk, wv)


def on_device(candidates, row_lengths, enc_bank, dec_bank, w_query, w_key, w_value):
    shards = lax.axis_size("dp")
    count = candidates.shape[0]
    bank = enc_bank.shape[0]
    width = enc_bank.shape[2]
    rows = bank * L
    pairs, facts, packed = pl.pallas_call(
        pack_kernel,
        out_shape=[
            jax.ShapeDtypeStruct((5, count), jnp.int32),
            jax.ShapeDtypeStruct((3,), jnp.int32),
            jax.ShapeDtypeStruct((2 * rows, width), jnp.bfloat16),
        ],
        in_specs=[SMEM, SMEM, HBM, HBM],
        out_specs=[SMEM, SMEM, VMEM],
        scratch_shapes=[
            pltpu.VMEM((2, rows, width), jnp.bfloat16),
            pltpu.SMEM((2, bank), jnp.int32),
            pltpu.SemaphoreType.DMA((2, bank)),
        ],
        compiler_params=pltpu.CompilerParams(vmem_limit_bytes=58 * 2**20),
    )(candidates.T, row_lengths.T, enc_bank.reshape(rows, width), dec_bank.reshape(rows, width))
    x1, x2, x3 = lax.switch(facts[0], [functools.partial(gather, size) for size in SIZES], packed)
    context = attend(facts, pairs, packed, x1, x2, x3, w_query, w_key, w_value)
    spread = lax.all_to_all(context.reshape(shards, count, 4 * width + HD), "dp", 0, 0, tiled=True)
    routed = pl.pallas_call(
        route_kernel,
        out_shape=jax.ShapeDtypeStruct((shards * GCAP, 4 * width), jnp.bfloat16),
        in_specs=[VMEM],
        out_specs=VMEM,
        compiler_params=pltpu.CompilerParams(vmem_limit_bytes=40 * 2**20),
    )(spread.reshape(shards * count, 4 * width + HD))
    arrived = lax.all_to_all(routed.reshape(shards, GCAP, 4 * width), "dp", 0, 0, tiled=True)
    return pl.pallas_call(
        place_kernel,
        grid=(4,),
        out_shape=jax.ShapeDtypeStruct((GCAP, L, width), jnp.bfloat16),
        in_specs=[pl.BlockSpec((shards * GCAP, width), lambda g: (0, g))],
        out_specs=pl.BlockSpec((GCAP, 32, width), lambda g: (0, g, 0)),
        scratch_shapes=[pltpu.VMEM((width // HD, shards * GCAP, HD), jnp.float32)],
        compiler_params=pltpu.CompilerParams(vmem_limit_bytes=40 * 2**20),
    )(arrived.reshape(shards * GCAP, 4 * width))


def solution(mesh):
    placed = (
        P("dp", None),
        P("dp", None),
        P("dp", None, "mp"),
        P("dp", None, "mp"),
        P(None, "mp"),
        P(None, "mp"),
        P(None, "mp"),
    )
    return jax.shard_map(on_device, mesh=mesh, in_specs=placed, out_specs=P("dp", None, "mp"), check_vma=False)
```

```python
import functools
import math

import jax
import jax.numpy as jnp
from jax import lax
from jax.experimental import pallas as pl
from jax.experimental.pallas import tpu as pltpu
from jax.sharding import PartitionSpec as P

D = 2048
HD = 128
L = 128
GCAP = 24
BLOCK = 16
BLOCKS = L // BLOCK
TILE = 256
SIZES = (1408, 1536, 1664, 1728, 1792, 1856, 1920, 2048, 2304, 4096)
VMEM = pl.BlockSpec(memory_space=pltpu.VMEM)
SMEM = pl.BlockSpec(memory_space=pltpu.SMEM)
HBM = pl.BlockSpec(memory_space=pltpu.HBM)


def pack_kernel(cand, lens, enc, dec, out_pairs, facts, out_hbm, out, staged, starts, arrived, left):
    rows = enc.shape[0] // L
    count = cand.shape[1]
    for row in range(rows):
        starts[0, row] = 0
        starts[1, row] = 0
    for c in range(count):
        starts[0, cand[0, c]] = 1
        starts[1, cand[1, c]] = 1
    banks = (enc, dec)

    def load(column, row):
        at = slice(row * L, (row + 1) * L)
        return pltpu.make_async_copy(banks[column].at[at], staged.at[column, at], arrived.at[column, row])

    for column in range(2):
        for row in range(rows):

            @pl.when(starts[column, row] > 0)
            def _(column=column, row=row):
                load(column, row).start()

    total = jnp.int32(0)
    for column in range(2):
        for row in range(rows):
            needed = starts[column, row] > 0
            blocks = jnp.where(needed, (lens[column, row] + BLOCK - 1) // BLOCK, 0)
            starts[column, row] = total * BLOCK

            @pl.when(needed)
            def _(column=column, row=row):
                load(column, row).wait()

            def move(b, carry, column=column, row=row, first=total):
                to = pl.multiple_of((first + b) * BLOCK, BLOCK)
                out[pl.ds(to, BLOCK), :] = staged[column, pl.ds(pl.multiple_of(row * L + b * BLOCK, BLOCK), BLOCK), :]
                return carry

            lax.fori_loop(0, blocks, move, 0)
            total = total + blocks
        facts[1 + column] = total * BLOCK
    bucket = jnp.int32(0)
    size = jnp.int32(SIZES[0])
    for low, high in zip(SIZES, SIZES[1:]):
        over = total * BLOCK > low
        bucket = bucket + over.astype(jnp.int32)
        size = jnp.where(over, high, size)
    facts[0] = bucket

    def place(c, carry):
        s, t = cand[0, c], cand[1, c]
        out_pairs[0, c] = starts[0, s]
        out_pairs[1, c] = starts[1, t]
        out_pairs[2, c] = lens[0, s]
        out_pairs[3, c] = lens[1, t]
        out_pairs[4, c] = cand[2, c]
        return carry

    lax.fori_loop(0, count, place, 0)

    def clear(b, carry):
        out[pl.ds(pl.multiple_of(b * BLOCK, BLOCK), BLOCK), :] = jnp.zeros((BLOCK, out.shape[1]), out.dtype)
        return carry

    lax.fori_loop(total, size // BLOCK, clear, 0)

    def leave(i):
        rows = pl.ds(pl.multiple_of(i * L, L), L)
        return pltpu.make_async_copy(out.at[rows], out_hbm.at[rows], left.at[i])

    def begin_leave(i, carry):
        leave(i).start()
        return carry

    def finish_leave(i, carry):
        leave(i).wait()
        return carry

    pieces = (size + L - 1) // L
    lax.fori_loop(0, pieces, begin_leave, 0)
    lax.fori_loop(0, pieces, finish_leave, 0)


def assemble_kernel(*refs):
    pieces, (out1, out2, out3, done) = refs[:6], refs[6:]
    half = pieces[0].shape[0]
    low, high = slice(0, half), slice(half, 2 * half)
    outs = (out1.at[low], out3.at[high], out1.at[high], out3.at[low], out2.at[low], out2.at[high])
    copies = [pltpu.make_async_copy(piece, out, done.at[k]) for k, (piece, out) in enumerate(zip(pieces, outs))]
    for copy in copies:
        copy.start()
    for copy in copies:
        copy.wait()


def attend_kernel(
    facts, pairs, x0, x1, x2, x3, wq_in, wk, wv_in, out, xs, wq, wv, keys, values, queries, turned, arrived, ready
):
    width = x0.shape[1]
    heads = width // HD
    me = lax.axis_index("mp")
    origin = [pl.multiple_of(lax.rem(me + (4 - d), 4) * width, width) for d in range(4)]
    source = pl.multiple_of(facts[1], BLOCK)
    target = facts[2] - facts[1]
    count = pairs.shape[1]
    chunks = (facts[2] + TILE - 1) // TILE
    tiles = (source + TILE - 1) // TILE

    def loads(i):
        rows = pl.ds(pl.multiple_of(i * TILE, TILE), TILE)
        return [
            pltpu.make_async_copy(x.at[rows], xs.at[d, rows], arrived.at[d, i]) for d, x in enumerate((x0, x1, x2, x3))
        ]

    def begin(i, carry):
        for copy in loads(i):
            copy.start()
        return carry

    def finish(i, carry):
        for copy in loads(i):
            copy.wait()
        return carry

    value_load = pltpu.make_async_copy(wv_in, wv, ready.at[0])
    query_load = pltpu.make_async_copy(wq_in, wq, ready.at[1])
    begin(0, 0)
    value_load.start()
    lax.fori_loop(1, chunks, begin, 0)
    query_load.start()

    def project(i, weight, out):
        rows = pl.ds(pl.multiple_of(i * TILE, TILE), TILE)
        total = jnp.zeros((TILE, width), jnp.float32)
        for d in range(4):
            total += jnp.dot(xs[d, rows, :], weight[pl.ds(origin[d], width), :], preferred_element_type=jnp.float32)
        out[rows, :] = total.astype(jnp.bfloat16)

    def key_tile(i, carry):
        finish(i, 0)
        project(i, wk, keys)
        return carry

    def value_tile(i, carry):
        project(i, wv, values)
        return carry

    lax.fori_loop(0, tiles, key_tile, 0)
    value_load.wait()
    lax.fori_loop(0, tiles, value_tile, 0)
    values[pl.ds(source, L), :] = jnp.zeros((L, width), jnp.bfloat16)
    lax.fori_loop(tiles, chunks, finish, 0)
    query_load.wait()

    def q_tile(i, carry):
        rows = pl.ds(pl.multiple_of(source + i * TILE, BLOCK), TILE)
        wide = [xs[d, rows, :].astype(jnp.float32) for d in range(4)]
        mean = sum(jnp.sum(x, axis=-1, keepdims=True) for x in wide) * (1.0 / D)
        wide = [x - mean for x in wide]
        variance = sum(jnp.sum(x * x, axis=-1, keepdims=True) for x in wide) * (1.0 / D)
        scale = lax.rsqrt(variance + 1e-05)
        total = jnp.zeros((TILE, width), jnp.float32)
        for x, start in zip(wide, origin):
            total += jnp.dot(
                (x * scale).astype(jnp.bfloat16), wq[pl.ds(start, width), :], preferred_element_type=jnp.float32
            )
        queries[pl.ds(pl.multiple_of(i * TILE, TILE), TILE), :] = total.astype(jnp.bfloat16)
        return carry

    lax.fori_loop(0, (target + TILE - 1) // TILE, q_tile, 0)
    column = lax.broadcasted_iota(jnp.int32, (L, L), 1)
    line = lax.broadcasted_iota(jnp.int32, (L, HD), 0)

    def pair(p, carry):
        s_at = pl.multiple_of(pairs[0, p], BLOCK)
        t_at = pl.multiple_of(pairs[1, p] - source, BLOCK)
        key_mask = column < pairs[2, p]
        query_mask = line < pairs[3, p]
        cols = [slice(h * HD, (h + 1) * HD) for h in range(heads)]
        scores = [
            lax.dot_general(
                queries[pl.ds(t_at, L), c],
                keys[pl.ds(s_at, L), c],
                (((1,), (1,)), ((), ())),
                preferred_element_type=jnp.float32,
            )
            for c in cols
        ]
        scores = [jnp.where(key_mask, s * (1.0 / math.sqrt(HD)), -1e30) for s in scores]
        tops = [jnp.max(s, axis=-1, keepdims=True) for s in scores]
        terms = [jnp.exp(s - top) for s, top in zip(scores, tops)]
        sums = [jnp.sum(t, axis=-1, keepdims=True) for t in terms]
        weights = [(t * (1.0 / total)).astype(jnp.bfloat16) for t, total in zip(terms, sums)]
        contexts = [
            jnp.dot(w, values[pl.ds(s_at, L), c], preferred_element_type=jnp.float32)
            for w, c in zip(weights, cols)
        ]
        for h, context in enumerate(contexts):
            context = jnp.where(query_mask, context, 0.0)
            for g in range(4):
                turned[h + g * heads, pl.ds(p, 32, stride=count), :] = context[g * 32 : (g + 1) * 32]
        return carry

    lax.fori_loop(0, count, pair, 0, unroll=4)
    for k in range(4 * heads):
        g, h = k // heads, k % heads
        at = g * width + h * HD
        out[:, at : at + HD] = turned[k].astype(jnp.bfloat16)
    line = lax.broadcasted_iota(jnp.int32, (count, HD), 0)
    groups = jnp.zeros((count, HD), jnp.float32)
    for p in range(count):
        groups = jnp.where(line == p, pairs[4, p].astype(jnp.float32), groups)
    for j in range(32):
        out[j * count : (j + 1) * count, 4 * width :] = groups.astype(jnp.bfloat16)


def route_kernel(x, out):
    total = x.shape[0]
    width = out.shape[1]
    mine = x[:, width : width + 1].astype(jnp.float32)
    a = lax.broadcasted_iota(jnp.int32, (total, total), 0)
    b = lax.broadcasted_iota(jnp.int32, (total, total), 1)
    ones = jnp.ones((16, total), jnp.bfloat16)
    spread = jnp.where(a == b, mine, 0.0).astype(jnp.bfloat16)
    group = jnp.dot(ones, spread, preferred_element_type=jnp.float32)[:1]
    before = jnp.where((mine == group) & (a < b), 1.0, 0.0).astype(jnp.bfloat16)
    rank = jnp.dot(ones, before, preferred_element_type=jnp.float32)[:1]
    slot = (group * GCAP + rank).astype(jnp.int32)
    choose = lax.broadcasted_iota(jnp.int32, (out.shape[0], total), 0) == slot
    choose = jnp.where(choose, 1.0, 0.0).astype(jnp.bfloat16)
    for c in range(0, width, 256):
        out[:, c : c + 256] = jnp.dot(choose, x[:, c : c + 256], preferred_element_type=jnp.float32).astype(
            jnp.bfloat16
        )


def place_kernel(x, out, wide):
    slots, pieces, width = out.shape
    for c in range(width // HD):
        cols = slice(c * HD, (c + 1) * HD)
        wide[c] = x[:, cols].astype(jnp.float32)
    for q in range(slots):
        for c in range(width // HD):
            out[q, :, c * HD : (c + 1) * HD] = wide[c, pl.ds(q, pieces, stride=slots), :].astype(jnp.bfloat16)


def gather(size, packed):
    half = size // 2
    send = lambda x, step: lax.ppermute(x, "mp", [(i, (i + step) % 4) for i in range(4)])
    low, high = packed[:half], packed[half:size]
    left, right = send(low, 1), send(high, 3)
    pieces = [left, right, send(high, 1), send(low, 3), send(left, 1), send(right, 3)]
    return pl.pallas_call(
        assemble_kernel,
        out_shape=[jax.ShapeDtypeStruct(packed.shape, jnp.bfloat16)] * 3,
        in_specs=[VMEM] * 6,
        out_specs=[HBM] * 3,
        scratch_shapes=[pltpu.SemaphoreType.DMA((6,))],
        compiler_params=pltpu.CompilerParams(vmem_limit_bytes=13 * 2**20),
    )(*pieces)


def attend(facts, pairs, x0, x1, x2, x3, wq, wk, wv):
    total, width = x0.shape
    rows = total // 2 - TILE // 2
    n = pairs.shape[1] * 32
    return pl.pallas_call(
        attend_kernel,
        out_shape=jax.ShapeDtypeStruct((n, 4 * width + HD), jnp.bfloat16),
        in_specs=[SMEM, SMEM] + [HBM] * 5 + [VMEM, HBM],
        out_specs=VMEM,
        scratch_shapes=[
            pltpu.VMEM((4, total, width), jnp.bfloat16),
            pltpu.VMEM((D, width), jnp.bfloat16),
            pltpu.VMEM((D, width), jnp.bfloat16),
            pltpu.VMEM((rows + L, width), jnp.bfloat16),
            pltpu.VMEM((rows + L, width), jnp.bfloat16),
            pltpu.VMEM((rows + L, width), jnp.bfloat16),
            pltpu.VMEM((4 * width // HD, n, HD), jnp.float32),
            pltpu.SemaphoreType.DMA((4, total // TILE)),
            pltpu.SemaphoreType.DMA((2,)),
        ],
        compiler_params=pltpu.CompilerParams(vmem_limit_bytes=54 * 2**20),
    )(facts, pairs, x0, x1, x2, x3, wq, wk, wv)


def on_device(candidates, row_lengths, enc_bank, dec_bank, w_query, w_key, w_value):
    shards = lax.axis_size("dp")
    count = candidates.shape[0]
    bank = enc_bank.shape[0]
    width = enc_bank.shape[2]
    rows = bank * L
    pairs, facts, packed = pl.pallas_call(
        pack_kernel,
        out_shape=[
            jax.ShapeDtypeStruct((5, count), jnp.int32),
            jax.ShapeDtypeStruct((3,), jnp.int32),
            jax.ShapeDtypeStruct((2 * rows + TILE, width), jnp.bfloat16),
        ],
        in_specs=[SMEM, SMEM, HBM, HBM],
        out_specs=[SMEM, SMEM, HBM],
        scratch_shapes=[
            pltpu.VMEM((2 * rows + TILE, width), jnp.bfloat16),
            pltpu.VMEM((2, rows, width), jnp.bfloat16),
            pltpu.SMEM((2, bank), jnp.int32),
            pltpu.SemaphoreType.DMA((2, bank)),
            pltpu.SemaphoreType.DMA((2 * bank + TILE // L,)),
        ],
        compiler_params=pltpu.CompilerParams(vmem_limit_bytes=58 * 2**20),
    )(candidates.T, row_lengths.T, enc_bank.reshape(rows, width), dec_bank.reshape(rows, width))
    x1, x2, x3 = lax.switch(facts[0], [functools.partial(gather, size) for size in SIZES], packed)
    context = attend(facts, pairs, packed, x1, x2, x3, w_query, w_key, w_value)
    spread = lax.all_to_all(context.reshape(shards, count, 4 * width + HD), "dp", 0, 0, tiled=True)
    routed = pl.pallas_call(
        route_kernel,
        out_shape=jax.ShapeDtypeStruct((shards * GCAP, 4 * width), jnp.bfloat16),
        in_specs=[VMEM],
        out_specs=VMEM,
        compiler_params=pltpu.CompilerParams(vmem_limit_bytes=40 * 2**20),
    )(spread.reshape(shards * count, 4 * width + HD))
    arrived = lax.all_to_all(routed.reshape(shards, GCAP, 4 * width), "dp", 0, 0, tiled=True)
    return pl.pallas_call(
        place_kernel,
        grid=(4,),
        out_shape=jax.ShapeDtypeStruct((GCAP, L, width), jnp.bfloat16),
        in_specs=[pl.BlockSpec((shards * GCAP, width), lambda g: (0, g))],
        out_specs=pl.BlockSpec((GCAP, 32, width), lambda g: (0, g, 0)),
        scratch_shapes=[pltpu.VMEM((width // HD, shards * GCAP, HD), jnp.float32)],
        compiler_params=pltpu.CompilerParams(vmem_limit_bytes=40 * 2**20),
    )(arrived.reshape(shards * GCAP, 4 * width))


def solution(mesh):
    placed = (
        P("dp", None),
        P("dp", None),
        P("dp", None, "mp"),
        P("dp", None, "mp"),
        P(None, "mp"),
        P(None, "mp"),
        P(None, "mp"),
    )
    return jax.shard_map(on_device, mesh=mesh, in_specs=placed, out_specs=P("dp", None, "mp"), check_vma=False)
```

```python
import functools
import math

import jax
import jax.numpy as jnp
from jax import lax
from jax.experimental import pallas as pl
from jax.experimental.pallas import tpu as pltpu
from jax.sharding import PartitionSpec as P

D = 2048
HD = 128
L = 128
GCAP = 24
BLOCK = 16
BLOCKS = L // BLOCK
TILE = 256
SIZES = (1408, 1536, 1664, 1728, 1792, 1856, 1920, 2048, 2304, 4096)
VMEM = pl.BlockSpec(memory_space=pltpu.VMEM)
SMEM = pl.BlockSpec(memory_space=pltpu.SMEM)
HBM = pl.BlockSpec(memory_space=pltpu.HBM)


def pack_kernel(cand, lens, enc, dec, out_pairs, facts, out, out_hbm, staged, starts, arrived, left):
    rows = enc.shape[0] // L
    count = cand.shape[1]
    for row in range(rows):
        starts[0, row] = 0
        starts[1, row] = 0
    for c in range(count):
        starts[0, cand[0, c]] = 1
        starts[1, cand[1, c]] = 1
    banks = (enc, dec)

    def load(column, row):
        at = slice(row * L, (row + 1) * L)
        return pltpu.make_async_copy(banks[column].at[at], staged.at[column, at], arrived.at[column, row])

    for column in range(2):
        for row in range(rows):

            @pl.when(starts[column, row] > 0)
            def _(column=column, row=row):
                load(column, row).start()

    total = jnp.int32(0)
    for column in range(2):
        for row in range(rows):
            needed = starts[column, row] > 0
            blocks = jnp.where(needed, (lens[column, row] + BLOCK - 1) // BLOCK, 0)
            starts[column, row] = total * BLOCK

            @pl.when(needed)
            def _(column=column, row=row, first=total):
                load(column, row).wait()
                to = pl.multiple_of(first * BLOCK, BLOCK)
                out[pl.ds(to, L), :] = staged[column, row * L : (row + 1) * L, :]

            total = total + blocks
        facts[1 + column] = total * BLOCK
    bucket = jnp.int32(0)
    size = jnp.int32(SIZES[0])
    for low, high in zip(SIZES, SIZES[1:]):
        over = total * BLOCK > low
        bucket = bucket + over.astype(jnp.int32)
        size = jnp.where(over, high, size)
    facts[0] = bucket

    def place(c, carry):
        s, t = cand[0, c], cand[1, c]
        out_pairs[0, c] = starts[0, s]
        out_pairs[1, c] = starts[1, t]
        out_pairs[2, c] = lens[0, s]
        out_pairs[3, c] = lens[1, t]
        out_pairs[4, c] = cand[2, c]
        return carry

    lax.fori_loop(0, count, place, 0)

    def leave(i):
        rows = pl.ds(pl.multiple_of(i * L, L), L)
        return pltpu.make_async_copy(out.at[rows], out_hbm.at[rows], left.at[i])

    def begin_leave(i, carry):
        leave(i).start()
        return carry

    def finish_leave(i, carry):
        leave(i).wait()
        return carry

    pieces = (size + L - 1) // L
    lax.fori_loop(0, pieces, begin_leave, 0)
    lax.fori_loop(0, pieces, finish_leave, 0)


def assemble_kernel(*refs):
    pieces, (out1, out2, out3, done) = refs[:6], refs[6:]
    half = pieces[0].shape[0]
    low, high = slice(0, half), slice(half, 2 * half)
    outs = (out1.at[low], out3.at[high], out1.at[high], out3.at[low], out2.at[low], out2.at[high])
    copies = [pltpu.make_async_copy(piece, out, done.at[k]) for k, (piece, out) in enumerate(zip(pieces, outs))]
    for copy in copies:
        copy.start()
    for copy in copies:
        copy.wait()


def attend_kernel(
    facts, pairs, x0, x1, x2, x3, wk, wv_in, wq_in, out, xs, wq, wv, keys, values, queries, turned, arrived, ready
):
    width = x0.shape[1]
    heads = width // HD
    me = lax.axis_index("mp")
    origin = [pl.multiple_of(lax.rem(me + (4 - d), 4) * width, width) for d in range(4)]
    source = pl.multiple_of(facts[1], BLOCK)
    target = facts[2] - facts[1]
    count = pairs.shape[1]
    chunks = (facts[2] + TILE - 1) // TILE
    tiles = (source + TILE - 1) // TILE

    def loads(i):
        rows = pl.ds(pl.multiple_of(i * TILE, TILE), TILE)
        return [
            pltpu.make_async_copy(x.at[rows], xs.at[d, rows], arrived.at[d, i]) for d, x in enumerate((x0, x1, x2, x3))
        ]

    def begin(i, carry):
        for copy in loads(i):
            copy.start()
        return carry

    def finish(i, carry):
        for copy in loads(i):
            copy.wait()
        return carry

    value_load = pltpu.make_async_copy(wv_in, wv, ready.at[0])
    query_load = pltpu.make_async_copy(wq_in, wq, ready.at[1])
    begin(0, 0)
    value_load.start()
    lax.fori_loop(1, chunks, begin, 0)
    query_load.start()

    def project(i, weight, out):
        rows = pl.ds(pl.multiple_of(i * TILE, TILE), TILE)
        total = jnp.zeros((TILE, width), jnp.float32)
        for d in range(4):
            total += jnp.dot(xs[d, rows, :], weight[pl.ds(origin[d], width), :], preferred_element_type=jnp.float32)
        out[rows, :] = total.astype(jnp.bfloat16)

    def key_tile(i, carry):
        finish(i, 0)
        project(i, wk, keys)
        return carry

    def value_tile(i, carry):
        project(i, wv, values)
        return carry

    lax.fori_loop(0, tiles, key_tile, 0)
    value_load.wait()
    lax.fori_loop(0, tiles, value_tile, 0)
    values[pl.ds(source, L), :] = jnp.zeros((L, width), jnp.bfloat16)
    lax.fori_loop(tiles, chunks, finish, 0)
    query_load.wait()

    def q_tile(i, carry):
        rows = pl.ds(pl.multiple_of(source + i * TILE, BLOCK), TILE)
        wide = [xs[d, rows, :].astype(jnp.float32) for d in range(4)]
        mean = sum(jnp.sum(x, axis=-1, keepdims=True) for x in wide) * (1.0 / D)
        wide = [x - mean for x in wide]
        variance = sum(jnp.sum(x * x, axis=-1, keepdims=True) for x in wide) * (1.0 / D)
        scale = lax.rsqrt(variance + 1e-05)
        total = jnp.zeros((TILE, width), jnp.float32)
        for x, start in zip(wide, origin):
            total += jnp.dot(
                (x * scale).astype(jnp.bfloat16), wq[pl.ds(start, width), :], preferred_element_type=jnp.float32
            )
        queries[pl.ds(pl.multiple_of(i * TILE, TILE), TILE), :] = total.astype(jnp.bfloat16)
        return carry

    lax.fori_loop(0, (target + TILE - 1) // TILE, q_tile, 0)
    column = lax.broadcasted_iota(jnp.int32, (L, L), 1)
    line = lax.broadcasted_iota(jnp.int32, (L, HD), 0)

    def pair(p, carry):
        s_at = pl.multiple_of(pairs[0, p], BLOCK)
        t_at = pl.multiple_of(pairs[1, p] - source, BLOCK)
        key_mask = column < pairs[2, p]
        query_mask = line < pairs[3, p]
        cols = [slice(h * HD, (h + 1) * HD) for h in range(heads)]
        scores = [
            lax.dot_general(
                queries[pl.ds(t_at, L), c],
                keys[pl.ds(s_at, L), c],
                (((1,), (1,)), ((), ())),
                preferred_element_type=jnp.float32,
            )
            for c in cols
        ]
        scores = [jnp.where(key_mask, s * (1.0 / math.sqrt(HD)), -1e30) for s in scores]
        tops = [jnp.max(s, axis=-1, keepdims=True) for s in scores]
        terms = [jnp.exp(s - top) for s, top in zip(scores, tops)]
        sums = [jnp.sum(t, axis=-1, keepdims=True) for t in terms]
        weights = [(t * (1.0 / total)).astype(jnp.bfloat16) for t, total in zip(terms, sums)]
        contexts = [
            jnp.dot(w, values[pl.ds(s_at, L), c], preferred_element_type=jnp.float32)
            for w, c in zip(weights, cols)
        ]
        for h, context in enumerate(contexts):
            context = jnp.where(query_mask, context, 0.0)
            for g in range(4):
                turned[h + g * heads, pl.ds(p, 32, stride=count), :] = context[g * 32 : (g + 1) * 32]
        return carry

    lax.fori_loop(0, count, pair, 0, unroll=4)
    for k in range(4 * heads):
        g, h = k // heads, k % heads
        at = g * width + h * HD
        out[:, at : at + HD] = turned[k].astype(jnp.bfloat16)
    line = lax.broadcasted_iota(jnp.int32, (count, HD), 0)
    groups = jnp.zeros((count, HD), jnp.float32)
    for p in range(count):
        groups = jnp.where(line == p, pairs[4, p].astype(jnp.float32), groups)
    for j in range(32):
        out[j * count : (j + 1) * count, 4 * width :] = groups.astype(jnp.bfloat16)


def route_kernel(x, out):
    total = x.shape[0]
    width = out.shape[1]
    mine = x[:, width : width + 1].astype(jnp.float32)
    a = lax.broadcasted_iota(jnp.int32, (total, total), 0)
    b = lax.broadcasted_iota(jnp.int32, (total, total), 1)
    ones = jnp.ones((16, total), jnp.bfloat16)
    spread = jnp.where(a == b, mine, 0.0).astype(jnp.bfloat16)
    group = jnp.dot(ones, spread, preferred_element_type=jnp.float32)[:1]
    before = jnp.where((mine == group) & (a < b), 1.0, 0.0).astype(jnp.bfloat16)
    rank = jnp.dot(ones, before, preferred_element_type=jnp.float32)[:1]
    slot = (group * GCAP + rank).astype(jnp.int32)
    choose = lax.broadcasted_iota(jnp.int32, (out.shape[0], total), 0) == slot
    choose = jnp.where(choose, 1.0, 0.0).astype(jnp.bfloat16)
    for c in range(0, width, 256):
        out[:, c : c + 256] = jnp.dot(choose, x[:, c : c + 256], preferred_element_type=jnp.float32).astype(
            jnp.bfloat16
        )


def place_kernel(x, out, wide):
    slots, pieces, width = out.shape
    for c in range(width // HD):
        cols = slice(c * HD, (c + 1) * HD)
        wide[c] = x[:, cols].astype(jnp.float32)
    for q in range(slots):
        for c in range(width // HD):
            out[q, :, c * HD : (c + 1) * HD] = wide[c, pl.ds(q, pieces, stride=slots), :].astype(jnp.bfloat16)


def gather(size, packed):
    half = size // 2
    send = lambda x, step: lax.ppermute(x, "mp", [(i, (i + step) % 4) for i in range(4)])
    low, high = packed[:half], packed[half:size]
    left, right = send(low, 1), send(high, 3)
    pieces = [left, right, send(high, 1), send(low, 3), send(left, 1), send(right, 3)]
    return pl.pallas_call(
        assemble_kernel,
        out_shape=[jax.ShapeDtypeStruct(packed.shape, jnp.bfloat16)] * 3,
        in_specs=[VMEM] * 6,
        out_specs=[HBM] * 3,
        scratch_shapes=[pltpu.SemaphoreType.DMA((6,))],
        compiler_params=pltpu.CompilerParams(vmem_limit_bytes=13 * 2**20),
    )(*pieces)


def attend(facts, pairs, x0, x1, x2, x3, wq, wk, wv):
    total, width = x0.shape
    rows = total // 2 - TILE // 2
    n = pairs.shape[1] * 32
    return pl.pallas_call(
        attend_kernel,
        out_shape=jax.ShapeDtypeStruct((n, 4 * width + HD), jnp.bfloat16),
        in_specs=[SMEM, SMEM] + [HBM] * 4 + [VMEM, HBM, HBM],
        out_specs=VMEM,
        scratch_shapes=[
            pltpu.VMEM((4, total, width), jnp.bfloat16),
            pltpu.VMEM((D, width), jnp.bfloat16),
            pltpu.VMEM((D, width), jnp.bfloat16),
            pltpu.VMEM((rows + L, width), jnp.bfloat16),
            pltpu.VMEM((rows + L, width), jnp.bfloat16),
            pltpu.VMEM((rows + L, width), jnp.bfloat16),
            pltpu.VMEM((4 * width // HD, n, HD), jnp.float32),
            pltpu.SemaphoreType.DMA((4, total // TILE)),
            pltpu.SemaphoreType.DMA((2,)),
        ],
        compiler_params=pltpu.CompilerParams(vmem_limit_bytes=54 * 2**20),
    )(facts, pairs, x0, x1, x2, x3, wk, wv, wq)


def on_device(candidates, row_lengths, enc_bank, dec_bank, w_query, w_key, w_value):
    shards = lax.axis_size("dp")
    count = candidates.shape[0]
    bank = enc_bank.shape[0]
    width = enc_bank.shape[2]
    rows = bank * L
    pairs, facts, packed, kept = pl.pallas_call(
        pack_kernel,
        out_shape=[
            jax.ShapeDtypeStruct((5, count), jnp.int32),
            jax.ShapeDtypeStruct((3,), jnp.int32),
            jax.ShapeDtypeStruct((2 * rows + TILE, width), jnp.bfloat16),
            jax.ShapeDtypeStruct((2 * rows + TILE, width), jnp.bfloat16),
        ],
        in_specs=[SMEM, SMEM, HBM, HBM],
        out_specs=[SMEM, SMEM, VMEM, HBM],
        scratch_shapes=[
            pltpu.VMEM((2, rows, width), jnp.bfloat16),
            pltpu.SMEM((2, bank), jnp.int32),
            pltpu.SemaphoreType.DMA((2, bank)),
            pltpu.SemaphoreType.DMA((2 * bank + TILE // L,)),
        ],
        compiler_params=pltpu.CompilerParams(vmem_limit_bytes=58 * 2**20),
    )(candidates.T, row_lengths.T, enc_bank.reshape(rows, width), dec_bank.reshape(rows, width))
    x1, x2, x3 = lax.switch(facts[0], [functools.partial(gather, size) for size in SIZES], packed)
    context = attend(facts, pairs, kept, x1, x2, x3, w_query, w_key, w_value)
    spread = lax.all_to_all(context.reshape(shards, count, 4 * width + HD), "dp", 0, 0, tiled=True)
    routed = pl.pallas_call(
        route_kernel,
        out_shape=jax.ShapeDtypeStruct((shards * GCAP, 4 * width), jnp.bfloat16),
        in_specs=[VMEM],
        out_specs=VMEM,
        compiler_params=pltpu.CompilerParams(vmem_limit_bytes=40 * 2**20),
    )(spread.reshape(shards * count, 4 * width + HD))
    arrived = lax.all_to_all(routed.reshape(shards, GCAP, 4 * width), "dp", 0, 0, tiled=True)
    return pl.pallas_call(
        place_kernel,
        grid=(4,),
        out_shape=jax.ShapeDtypeStruct((GCAP, L, width), jnp.bfloat16),
        in_specs=[pl.BlockSpec((shards * GCAP, width), lambda g: (0, g))],
        out_specs=pl.BlockSpec((GCAP, 32, width), lambda g: (0, g, 0)),
        scratch_shapes=[pltpu.VMEM((width // HD, shards * GCAP, HD), jnp.float32)],
        compiler_params=pltpu.CompilerParams(vmem_limit_bytes=40 * 2**20),
    )(arrived.reshape(shards * GCAP, 4 * width))


def solution(mesh):
    placed = (
        P("dp", None),
        P("dp", None),
        P("dp", None, "mp"),
        P("dp", None, "mp"),
        P(None, "mp"),
        P(None, "mp"),
        P(None, "mp"),
    )
    return jax.shard_map(on_device, mesh=mesh, in_specs=placed, out_specs=P("dp", None, "mp"), check_vma=False)
```

```python
import functools
import math

import jax
import jax.numpy as jnp
from jax import lax
from jax.experimental import pallas as pl
from jax.experimental.pallas import tpu as pltpu
from jax.sharding import PartitionSpec as P

D = 2048
HD = 128
L = 128
GCAP = 24
BLOCK = 16
BLOCKS = L // BLOCK
TILE = 256
SIZES = (1408, 1536, 1664, 1728, 1792, 1856, 1920, 2048, 2304, 4096)
VMEM = pl.BlockSpec(memory_space=pltpu.VMEM)
SMEM = pl.BlockSpec(memory_space=pltpu.SMEM)
HBM = pl.BlockSpec(memory_space=pltpu.HBM)


def pack_kernel(cand, lens, enc, dec, out_pairs, facts, out, out_hbm, staged, starts, arrived, left):
    rows = enc.shape[0] // L
    count = cand.shape[1]
    for row in range(rows):
        starts[0, row] = 0
        starts[1, row] = 0
    for c in range(count):
        starts[0, cand[0, c]] = 1
        starts[1, cand[1, c]] = 1
    banks = (enc, dec)

    def load(column, row):
        at = slice(row * L, (row + 1) * L)
        return pltpu.make_async_copy(banks[column].at[at], staged.at[column, at], arrived.at[column, row])

    for column in range(2):
        for row in range(rows):

            @pl.when(starts[column, row] > 0)
            def _(column=column, row=row):
                load(column, row).start()

    total = jnp.int32(0)
    for column in range(2):
        for row in range(rows):
            needed = starts[column, row] > 0
            blocks = jnp.where(needed, (lens[column, row] + BLOCK - 1) // BLOCK, 0)
            starts[column, row] = total * BLOCK

            @pl.when(needed)
            def _(column=column, row=row, first=total):
                load(column, row).wait()
                to = pl.multiple_of(first * BLOCK, BLOCK)
                out[pl.ds(to, L), :] = staged[column, row * L : (row + 1) * L, :]

            total = total + blocks
        facts[1 + column] = total * BLOCK
    bucket = jnp.int32(0)
    size = jnp.int32(SIZES[0])
    for low, high in zip(SIZES, SIZES[1:]):
        over = total * BLOCK > low
        bucket = bucket + over.astype(jnp.int32)
        size = jnp.where(over, high, size)
    facts[0] = bucket

    def place(c, carry):
        s, t = cand[0, c], cand[1, c]
        out_pairs[0, c] = starts[0, s]
        out_pairs[1, c] = starts[1, t]
        out_pairs[2, c] = lens[0, s]
        out_pairs[3, c] = lens[1, t]
        out_pairs[4, c] = cand[2, c]
        return carry

    lax.fori_loop(0, count, place, 0)

    def leave(i):
        rows = pl.ds(pl.multiple_of(i * L, L), L)
        return pltpu.make_async_copy(out.at[rows], out_hbm.at[rows], left.at[i])

    def begin_leave(i, carry):
        leave(i).start()
        return carry

    def finish_leave(i, carry):
        leave(i).wait()
        return carry

    pieces = (size + L - 1) // L
    lax.fori_loop(0, pieces, begin_leave, 0)
    lax.fori_loop(0, pieces, finish_leave, 0)


def assemble_kernel(*refs):
    pieces, (out1, out2, out3, done) = refs[:6], refs[6:]
    half = pieces[0].shape[0]
    low, high = slice(0, half), slice(half, 2 * half)
    outs = (out1.at[low], out3.at[high], out1.at[high], out3.at[low], out2.at[low], out2.at[high])
    copies = [pltpu.make_async_copy(piece, out, done.at[k]) for k, (piece, out) in enumerate(zip(pieces, outs))]
    for copy in copies:
        copy.start()
    for copy in copies:
        copy.wait()


def attend_kernel(
    facts, pairs, x0, x1, x2, x3, wk, wv_in, wq_in, out, xs, wq, wv, keys, values, queries, turned, arrived, ready
):
    width = x0.shape[1]
    heads = width // HD
    me = lax.axis_index("mp")
    origin = [pl.multiple_of(lax.rem(me + (4 - d), 4) * width, width) for d in range(4)]
    source = pl.multiple_of(facts[1], BLOCK)
    target = facts[2] - facts[1]
    count = pairs.shape[1]
    chunks = (facts[2] + TILE - 1) // TILE
    tiles = (source + TILE - 1) // TILE

    def loads(i):
        rows = pl.ds(pl.multiple_of(i * TILE, TILE), TILE)
        return [
            pltpu.make_async_copy(x.at[rows], xs.at[d, rows], arrived.at[d, i]) for d, x in enumerate((x0, x1, x2, x3))
        ]

    def begin(i, carry):
        for copy in loads(i):
            copy.start()
        return carry

    def finish(i, carry):
        for copy in loads(i):
            copy.wait()
        return carry

    value_load = pltpu.make_async_copy(wv_in, wv, ready.at[0])
    query_load = pltpu.make_async_copy(wq_in, wq, ready.at[1])
    lax.fori_loop(0, tiles, begin, 0)
    value_load.start()
    lax.fori_loop(tiles, chunks, begin, 0)
    query_load.start()

    def project(i, weight, out):
        rows = pl.ds(pl.multiple_of(i * TILE, TILE), TILE)
        total = jnp.zeros((TILE, width), jnp.float32)
        for d in range(4):
            total += jnp.dot(xs[d, rows, :], weight[pl.ds(origin[d], width), :], preferred_element_type=jnp.float32)
        out[rows, :] = total.astype(jnp.bfloat16)

    def key_tile(i, carry):
        finish(i, 0)
        project(i, wk, keys)
        return carry

    def value_tile(i, carry):
        project(i, wv, values)
        return carry

    lax.fori_loop(0, tiles, key_tile, 0)
    value_load.wait()
    lax.fori_loop(0, tiles, value_tile, 0)
    values[pl.ds(source, L), :] = jnp.zeros((L, width), jnp.bfloat16)
    lax.fori_loop(tiles, chunks, finish, 0)
    query_load.wait()

    def q_tile(i, carry):
        rows = pl.ds(pl.multiple_of(source + i * TILE, BLOCK), TILE)
        wide = [xs[d, rows, :].astype(jnp.float32) for d in range(4)]
        mean = sum(jnp.sum(x, axis=-1, keepdims=True) for x in wide) * (1.0 / D)
        wide = [x - mean for x in wide]
        variance = sum(jnp.sum(x * x, axis=-1, keepdims=True) for x in wide) * (1.0 / D)
        scale = lax.rsqrt(variance + 1e-05)
        total = jnp.zeros((TILE, width), jnp.float32)
        for x, start in zip(wide, origin):
            total += jnp.dot(
                (x * scale).astype(jnp.bfloat16), wq[pl.ds(start, width), :], preferred_element_type=jnp.float32
            )
        queries[pl.ds(pl.multiple_of(i * TILE, TILE), TILE), :] = total.astype(jnp.bfloat16)
        return carry

    lax.fori_loop(0, (target + TILE - 1) // TILE, q_tile, 0)
    column = lax.broadcasted_iota(jnp.int32, (L, L), 1)
    line = lax.broadcasted_iota(jnp.int32, (L, HD), 0)

    def pair(p, carry):
        s_at = pl.multiple_of(pairs[0, p], BLOCK)
        t_at = pl.multiple_of(pairs[1, p] - source, BLOCK)
        key_mask = column < pairs[2, p]
        query_mask = line < pairs[3, p]
        cols = [slice(h * HD, (h + 1) * HD) for h in range(heads)]
        scores = [
            lax.dot_general(
                queries[pl.ds(t_at, L), c],
                keys[pl.ds(s_at, L), c],
                (((1,), (1,)), ((), ())),
                preferred_element_type=jnp.float32,
            )
            for c in cols
        ]
        scores = [jnp.where(key_mask, s * (1.0 / math.sqrt(HD)), -1e30) for s in scores]
        tops = [jnp.max(s, axis=-1, keepdims=True) for s in scores]
        terms = [jnp.exp(s - top) for s, top in zip(scores, tops)]
        sums = [jnp.sum(t, axis=-1, keepdims=True) for t in terms]
        weights = [(t * (1.0 / total)).astype(jnp.bfloat16) for t, total in zip(terms, sums)]
        contexts = [
            jnp.dot(w, values[pl.ds(s_at, L), c], preferred_element_type=jnp.float32)
            for w, c in zip(weights, cols)
        ]
        for h, context in enumerate(contexts):
            context = jnp.where(query_mask, context, 0.0)
            for g in range(4):
                turned[h + g * heads, pl.ds(p, 32, stride=count), :] = context[g * 32 : (g + 1) * 32]
        return carry

    lax.fori_loop(0, count, pair, 0, unroll=4)
    for k in range(4 * heads):
        g, h = k // heads, k % heads
        at = g * width + h * HD
        out[:, at : at + HD] = turned[k].astype(jnp.bfloat16)
    line = lax.broadcasted_iota(jnp.int32, (count, HD), 0)
    groups = jnp.zeros((count, HD), jnp.float32)
    for p in range(count):
        groups = jnp.where(line == p, pairs[4, p].astype(jnp.float32), groups)
    for j in range(32):
        out[j * count : (j + 1) * count, 4 * width :] = groups.astype(jnp.bfloat16)


def route_kernel(x, out):
    total = x.shape[0]
    width = out.shape[1]
    mine = x[:, width : width + 1].astype(jnp.float32)
    a = lax.broadcasted_iota(jnp.int32, (total, total), 0)
    b = lax.broadcasted_iota(jnp.int32, (total, total), 1)
    ones = jnp.ones((16, total), jnp.bfloat16)
    spread = jnp.where(a == b, mine, 0.0).astype(jnp.bfloat16)
    group = jnp.dot(ones, spread, preferred_element_type=jnp.float32)[:1]
    before = jnp.where((mine == group) & (a < b), 1.0, 0.0).astype(jnp.bfloat16)
    rank = jnp.dot(ones, before, preferred_element_type=jnp.float32)[:1]
    slot = (group * GCAP + rank).astype(jnp.int32)
    choose = lax.broadcasted_iota(jnp.int32, (out.shape[0], total), 0) == slot
    choose = jnp.where(choose, 1.0, 0.0).astype(jnp.bfloat16)
    for c in range(0, width, 256):
        out[:, c : c + 256] = jnp.dot(choose, x[:, c : c + 256], preferred_element_type=jnp.float32).astype(
            jnp.bfloat16
        )


def place_kernel(x, out, wide):
    slots, pieces, width = out.shape
    for c in range(width // HD):
        cols = slice(c * HD, (c + 1) * HD)
        wide[c] = x[:, cols].astype(jnp.float32)
    for q in range(slots):
        for c in range(width // HD):
            out[q, :, c * HD : (c + 1) * HD] = wide[c, pl.ds(q, pieces, stride=slots), :].astype(jnp.bfloat16)


def gather(size, packed):
    half = size // 2
    send = lambda x, step: lax.ppermute(x, "mp", [(i, (i + step) % 4) for i in range(4)])
    low, high = packed[:half], packed[half:size]
    left, right = send(low, 1), send(high, 3)
    pieces = [left, right, send(high, 1), send(low, 3), send(left, 1), send(right, 3)]
    return pl.pallas_call(
        assemble_kernel,
        out_shape=[jax.ShapeDtypeStruct(packed.shape, jnp.bfloat16)] * 3,
        in_specs=[VMEM] * 6,
        out_specs=[HBM] * 3,
        scratch_shapes=[pltpu.SemaphoreType.DMA((6,))],
        compiler_params=pltpu.CompilerParams(vmem_limit_bytes=13 * 2**20),
    )(*pieces)


def attend(facts, pairs, x0, x1, x2, x3, wq, wk, wv):
    total, width = x0.shape
    rows = total // 2 - TILE // 2
    n = pairs.shape[1] * 32
    return pl.pallas_call(
        attend_kernel,
        out_shape=jax.ShapeDtypeStruct((n, 4 * width + HD), jnp.bfloat16),
        in_specs=[SMEM, SMEM] + [HBM] * 4 + [VMEM, HBM, HBM],
        out_specs=VMEM,
        scratch_shapes=[
            pltpu.VMEM((4, total, width), jnp.bfloat16),
            pltpu.VMEM((D, width), jnp.bfloat16),
            pltpu.VMEM((D, width), jnp.bfloat16),
            pltpu.VMEM((rows + L, width), jnp.bfloat16),
            pltpu.VMEM((rows + L, width), jnp.bfloat16),
            pltpu.VMEM((rows + L, width), jnp.bfloat16),
            pltpu.VMEM((4 * width // HD, n, HD), jnp.float32),
            pltpu.SemaphoreType.DMA((4, total // TILE)),
            pltpu.SemaphoreType.DMA((2,)),
        ],
        compiler_params=pltpu.CompilerParams(vmem_limit_bytes=50 * 2**20),
    )(facts, pairs, x0, x1, x2, x3, wk, wv, wq)


def on_device(candidates, row_lengths, enc_bank, dec_bank, w_query, w_key, w_value):
    shards = lax.axis_size("dp")
    count = candidates.shape[0]
    bank = enc_bank.shape[0]
    width = enc_bank.shape[2]
    rows = bank * L
    pairs, facts, packed, kept = pl.pallas_call(
        pack_kernel,
        out_shape=[
            jax.ShapeDtypeStruct((5, count), jnp.int32),
            jax.ShapeDtypeStruct((3,), jnp.int32),
            jax.ShapeDtypeStruct((2 * rows + TILE, width), jnp.bfloat16),
            jax.ShapeDtypeStruct((2 * rows + TILE, width), jnp.bfloat16),
        ],
        in_specs=[SMEM, SMEM, HBM, HBM],
        out_specs=[SMEM, SMEM, VMEM, HBM],
        scratch_shapes=[
            pltpu.VMEM((2, rows, width), jnp.bfloat16),
            pltpu.SMEM((2, bank), jnp.int32),
            pltpu.SemaphoreType.DMA((2, bank)),
            pltpu.SemaphoreType.DMA((2 * bank + TILE // L,)),
        ],
        compiler_params=pltpu.CompilerParams(vmem_limit_bytes=56 * 2**20),
    )(candidates.T, row_lengths.T, enc_bank.reshape(rows, width), dec_bank.reshape(rows, width))
    x1, x2, x3 = lax.switch(facts[0], [functools.partial(gather, size) for size in SIZES], packed)
    context = attend(facts, pairs, kept, x1, x2, x3, w_query, w_key, w_value)
    spread = lax.all_to_all(context.reshape(shards, count, 4 * width + HD), "dp", 0, 0, tiled=True)
    routed = pl.pallas_call(
        route_kernel,
        out_shape=jax.ShapeDtypeStruct((shards * GCAP, 4 * width), jnp.bfloat16),
        in_specs=[VMEM],
        out_specs=VMEM,
        compiler_params=pltpu.CompilerParams(vmem_limit_bytes=40 * 2**20),
    )(spread.reshape(shards * count, 4 * width + HD))
    arrived = lax.all_to_all(routed.reshape(shards, GCAP, 4 * width), "dp", 0, 0, tiled=True)
    return pl.pallas_call(
        place_kernel,
        grid=(4,),
        out_shape=jax.ShapeDtypeStruct((GCAP, L, width), jnp.bfloat16),
        in_specs=[pl.BlockSpec((shards * GCAP, width), lambda g: (0, g))],
        out_specs=pl.BlockSpec((GCAP, 32, width), lambda g: (0, g, 0)),
        scratch_shapes=[pltpu.VMEM((width // HD, shards * GCAP, HD), jnp.float32)],
        compiler_params=pltpu.CompilerParams(vmem_limit_bytes=40 * 2**20),
    )(arrived.reshape(shards * GCAP, 4 * width))


def solution(mesh):
    placed = (
        P("dp", None),
        P("dp", None),
        P("dp", None, "mp"),
        P("dp", None, "mp"),
        P(None, "mp"),
        P(None, "mp"),
        P(None, "mp"),
    )
    return jax.shard_map(on_device, mesh=mesh, in_specs=placed, out_specs=P("dp", None, "mp"), check_vma=False)
```

```python
import functools
import math

import jax
import jax.numpy as jnp
from jax import lax
from jax.experimental import pallas as pl
from jax.experimental.pallas import tpu as pltpu
from jax.sharding import PartitionSpec as P

D = 2048
HD = 128
L = 128
GCAP = 24
BLOCK = 16
BLOCKS = L // BLOCK
TILE = 256
SIZES = (1408, 1536, 1664, 1728, 1792, 1856, 1920, 2048, 2304, 4096)
VMEM = pl.BlockSpec(memory_space=pltpu.VMEM)
SMEM = pl.BlockSpec(memory_space=pltpu.SMEM)
HBM = pl.BlockSpec(memory_space=pltpu.HBM)


def pack_kernel(cand, lens, enc, dec, out_pairs, facts, out, staged, starts, arrived):
    rows = enc.shape[0] // L
    count = cand.shape[1]
    for row in range(rows):
        starts[0, row] = 0
        starts[1, row] = 0
    for c in range(count):
        starts[0, cand[0, c]] = 1
        starts[1, cand[1, c]] = 1
    banks = (enc, dec)

    def load(column, row):
        at = slice(row * L, (row + 1) * L)
        return pltpu.make_async_copy(banks[column].at[at], staged.at[column, at], arrived.at[column, row])

    for column in range(2):
        for row in range(rows):

            @pl.when(starts[column, row] > 0)
            def _(column=column, row=row):
                load(column, row).start()

    total = jnp.int32(0)
    for column in range(2):
        for row in range(rows):
            needed = starts[column, row] > 0
            blocks = jnp.where(needed, (lens[column, row] + BLOCK - 1) // BLOCK, 0)
            starts[column, row] = total * BLOCK

            @pl.when(needed)
            def _(column=column, row=row, first=total):
                load(column, row).wait()
                to = pl.multiple_of(first * BLOCK, BLOCK)
                out[pl.ds(to, L), :] = staged[column, row * L : (row + 1) * L, :]

            total = total + blocks
        facts[1 + column] = total * BLOCK
    bucket = jnp.int32(0)
    for low in SIZES[:-1]:
        bucket = bucket + (total * BLOCK > low).astype(jnp.int32)
    facts[0] = bucket

    def place(c, carry):
        s, t = cand[0, c], cand[1, c]
        out_pairs[0, c] = starts[0, s]
        out_pairs[1, c] = starts[1, t]
        out_pairs[2, c] = lens[0, s]
        out_pairs[3, c] = lens[1, t]
        out_pairs[4, c] = cand[2, c]
        return carry

    lax.fori_loop(0, count, place, 0)


def assemble_kernel(*refs):
    pieces, (out0, out1, out2, out3, done) = refs[:8], refs[8:]
    half = pieces[0].shape[0]
    low, high = slice(0, half), slice(half, 2 * half)
    outs = (out1.at[low], out3.at[high], out1.at[high], out3.at[low], out2.at[low], out2.at[high], out0.at[low], out0.at[high])
    copies = [pltpu.make_async_copy(piece, out, done.at[k]) for k, (piece, out) in enumerate(zip(pieces, outs))]
    for copy in copies:
        copy.start()
    for copy in copies:
        copy.wait()


def attend_kernel(
    facts, pairs, x0, x1, x2, x3, wk, wv_in, wq_in, out, xs, wq, wv, keys, values, queries, turned, arrived, ready
):
    width = x0.shape[1]
    heads = width // HD
    me = lax.axis_index("mp")
    origin = [pl.multiple_of(lax.rem(me + (4 - d), 4) * width, width) for d in range(4)]
    source = pl.multiple_of(facts[1], BLOCK)
    target = facts[2] - facts[1]
    count = pairs.shape[1]
    chunks = (facts[2] + TILE - 1) // TILE
    tiles = (source + TILE - 1) // TILE

    def loads(i):
        rows = pl.ds(pl.multiple_of(i * TILE, TILE), TILE)
        return [
            pltpu.make_async_copy(x.at[rows], xs.at[d, rows], arrived.at[d, i]) for d, x in enumerate((x0, x1, x2, x3))
        ]

    def begin(i, carry):
        for copy in loads(i):
            copy.start()
        return carry

    def finish(i, carry):
        for copy in loads(i):
            copy.wait()
        return carry

    value_load = pltpu.make_async_copy(wv_in, wv, ready.at[0])
    query_load = pltpu.make_async_copy(wq_in, wq, ready.at[1])
    lax.fori_loop(0, tiles, begin, 0)
    value_load.start()
    lax.fori_loop(tiles, chunks, begin, 0)
    query_load.start()

    def project(i, weight, out):
        rows = pl.ds(pl.multiple_of(i * TILE, TILE), TILE)
        total = jnp.zeros((TILE, width), jnp.float32)
        for d in range(4):
            total += jnp.dot(xs[d, rows, :], weight[pl.ds(origin[d], width), :], preferred_element_type=jnp.float32)
        out[rows, :] = total.astype(jnp.bfloat16)

    def key_tile(i, carry):
        finish(i, 0)
        project(i, wk, keys)
        return carry

    def value_tile(i, carry):
        project(i, wv, values)
        return carry

    lax.fori_loop(0, tiles, key_tile, 0)
    value_load.wait()
    lax.fori_loop(0, tiles, value_tile, 0)
    values[pl.ds(source, L), :] = jnp.zeros((L, width), jnp.bfloat16)
    lax.fori_loop(tiles, chunks, finish, 0)
    query_load.wait()

    def q_tile(i, carry):
        rows = pl.ds(pl.multiple_of(source + i * TILE, BLOCK), TILE)
        wide = [xs[d, rows, :].astype(jnp.float32) for d in range(4)]
        mean = sum(jnp.sum(x, axis=-1, keepdims=True) for x in wide) * (1.0 / D)
        wide = [x - mean for x in wide]
        variance = sum(jnp.sum(x * x, axis=-1, keepdims=True) for x in wide) * (1.0 / D)
        scale = lax.rsqrt(variance + 1e-05)
        total = jnp.zeros((TILE, width), jnp.float32)
        for x, start in zip(wide, origin):
            total += jnp.dot(
                (x * scale).astype(jnp.bfloat16), wq[pl.ds(start, width), :], preferred_element_type=jnp.float32
            )
        queries[pl.ds(pl.multiple_of(i * TILE, TILE), TILE), :] = total.astype(jnp.bfloat16)
        return carry

    lax.fori_loop(0, (target + TILE - 1) // TILE, q_tile, 0)
    column = lax.broadcasted_iota(jnp.int32, (L, L), 1)
    line = lax.broadcasted_iota(jnp.int32, (L, HD), 0)

    def pair(p, carry):
        s_at = pl.multiple_of(pairs[0, p], BLOCK)
        t_at = pl.multiple_of(pairs[1, p] - source, BLOCK)
        key_mask = column < pairs[2, p]
        query_mask = line < pairs[3, p]
        cols = [slice(h * HD, (h + 1) * HD) for h in range(heads)]
        scores = [
            lax.dot_general(
                queries[pl.ds(t_at, L), c],
                keys[pl.ds(s_at, L), c],
                (((1,), (1,)), ((), ())),
                preferred_element_type=jnp.float32,
            )
            for c in cols
        ]
        scores = [jnp.where(key_mask, s * (1.0 / math.sqrt(HD)), -1e30) for s in scores]
        tops = [jnp.max(s, axis=-1, keepdims=True) for s in scores]
        terms = [jnp.exp(s - top) for s, top in zip(scores, tops)]
        sums = [jnp.sum(t, axis=-1, keepdims=True) for t in terms]
        weights = [(t * (1.0 / total)).astype(jnp.bfloat16) for t, total in zip(terms, sums)]
        contexts = [
            jnp.dot(w, values[pl.ds(s_at, L), c], preferred_element_type=jnp.float32)
            for w, c in zip(weights, cols)
        ]
        for h, context in enumerate(contexts):
            context = jnp.where(query_mask, context, 0.0)
            for g in range(4):
                turned[h + g * heads, pl.ds(p, 32, stride=count), :] = context[g * 32 : (g + 1) * 32]
        return carry

    lax.fori_loop(0, count, pair, 0, unroll=4)
    for k in range(4 * heads):
        g, h = k // heads, k % heads
        at = g * width + h * HD
        out[:, at : at + HD] = turned[k].astype(jnp.bfloat16)
    line = lax.broadcasted_iota(jnp.int32, (count, HD), 0)
    groups = jnp.zeros((count, HD), jnp.float32)
    for p in range(count):
        groups = jnp.where(line == p, pairs[4, p].astype(jnp.float32), groups)
    for j in range(32):
        out[j * count : (j + 1) * count, 4 * width :] = groups.astype(jnp.bfloat16)


def route_kernel(x, out):
    total = x.shape[0]
    width = out.shape[1]
    mine = x[:, width : width + 1].astype(jnp.float32)
    a = lax.broadcasted_iota(jnp.int32, (total, total), 0)
    b = lax.broadcasted_iota(jnp.int32, (total, total), 1)
    ones = jnp.ones((16, total), jnp.bfloat16)
    spread = jnp.where(a == b, mine, 0.0).astype(jnp.bfloat16)
    group = jnp.dot(ones, spread, preferred_element_type=jnp.float32)[:1]
    before = jnp.where((mine == group) & (a < b), 1.0, 0.0).astype(jnp.bfloat16)
    rank = jnp.dot(ones, before, preferred_element_type=jnp.float32)[:1]
    slot = (group * GCAP + rank).astype(jnp.int32)
    choose = lax.broadcasted_iota(jnp.int32, (out.shape[0], total), 0) == slot
    choose = jnp.where(choose, 1.0, 0.0).astype(jnp.bfloat16)
    for c in range(0, width, 256):
        out[:, c : c + 256] = jnp.dot(choose, x[:, c : c + 256], preferred_element_type=jnp.float32).astype(
            jnp.bfloat16
        )


def place_kernel(x, out, wide):
    slots, pieces, width = out.shape
    for c in range(width // HD):
        cols = slice(c * HD, (c + 1) * HD)
        wide[c] = x[:, cols].astype(jnp.float32)
    for q in range(slots):
        for c in range(width // HD):
            out[q, :, c * HD : (c + 1) * HD] = wide[c, pl.ds(q, pieces, stride=slots), :].astype(jnp.bfloat16)


def gather(size, packed):
    half = size // 2
    send = lambda x, step: lax.ppermute(x, "mp", [(i, (i + step) % 4) for i in range(4)])
    low, high = packed[:half], packed[half:size]
    left, right = send(low, 1), send(high, 3)
    pieces = [left, right, send(high, 1), send(low, 3), send(left, 1), send(right, 3), low, high]
    return pl.pallas_call(
        assemble_kernel,
        out_shape=[jax.ShapeDtypeStruct(packed.shape, jnp.bfloat16)] * 4,
        in_specs=[VMEM] * 8,
        out_specs=[HBM] * 4,
        scratch_shapes=[pltpu.SemaphoreType.DMA((8,))],
        compiler_params=pltpu.CompilerParams(vmem_limit_bytes=17 * 2**20),
    )(*pieces)


def attend(facts, pairs, x0, x1, x2, x3, wq, wk, wv):
    total, width = x0.shape
    rows = total // 2 - TILE // 2
    n = pairs.shape[1] * 32
    return pl.pallas_call(
        attend_kernel,
        out_shape=jax.ShapeDtypeStruct((n, 4 * width + HD), jnp.bfloat16),
        in_specs=[SMEM, SMEM] + [HBM] * 4 + [VMEM, HBM, HBM],
        out_specs=VMEM,
        scratch_shapes=[
            pltpu.VMEM((4, total, width), jnp.bfloat16),
            pltpu.VMEM((D, width), jnp.bfloat16),
            pltpu.VMEM((D, width), jnp.bfloat16),
            pltpu.VMEM((rows + L, width), jnp.bfloat16),
            pltpu.VMEM((rows + L, width), jnp.bfloat16),
            pltpu.VMEM((rows + L, width), jnp.bfloat16),
            pltpu.VMEM((4 * width // HD, n, HD), jnp.float32),
            pltpu.SemaphoreType.DMA((4, total // TILE)),
            pltpu.SemaphoreType.DMA((2,)),
        ],
        compiler_params=pltpu.CompilerParams(vmem_limit_bytes=50 * 2**20),
    )(facts, pairs, x0, x1, x2, x3, wk, wv, wq)


def on_device(candidates, row_lengths, enc_bank, dec_bank, w_query, w_key, w_value):
    shards = lax.axis_size("dp")
    count = candidates.shape[0]
    bank = enc_bank.shape[0]
    width = enc_bank.shape[2]
    rows = bank * L
    pairs, facts, packed = pl.pallas_call(
        pack_kernel,
        out_shape=[
            jax.ShapeDtypeStruct((5, count), jnp.int32),
            jax.ShapeDtypeStruct((3,), jnp.int32),
            jax.ShapeDtypeStruct((2 * rows + TILE, width), jnp.bfloat16),
        ],
        in_specs=[SMEM, SMEM, HBM, HBM],
        out_specs=[SMEM, SMEM, VMEM],
        scratch_shapes=[
            pltpu.VMEM((2, rows, width), jnp.bfloat16),
            pltpu.SMEM((2, bank), jnp.int32),
            pltpu.SemaphoreType.DMA((2, bank)),
        ],
        compiler_params=pltpu.CompilerParams(vmem_limit_bytes=56 * 2**20),
    )(candidates.T, row_lengths.T, enc_bank.reshape(rows, width), dec_bank.reshape(rows, width))
    x0, x1, x2, x3 = lax.switch(facts[0], [functools.partial(gather, size) for size in SIZES], packed)
    context = attend(facts, pairs, x0, x1, x2, x3, w_query, w_key, w_value)
    spread = lax.all_to_all(context.reshape(shards, count, 4 * width + HD), "dp", 0, 0, tiled=True)
    routed = pl.pallas_call(
        route_kernel,
        out_shape=jax.ShapeDtypeStruct((shards * GCAP, 4 * width), jnp.bfloat16),
        in_specs=[VMEM],
        out_specs=VMEM,
        compiler_params=pltpu.CompilerParams(vmem_limit_bytes=40 * 2**20),
    )(spread.reshape(shards * count, 4 * width + HD))
    arrived = lax.all_to_all(routed.reshape(shards, GCAP, 4 * width), "dp", 0, 0, tiled=True)
    return pl.pallas_call(
        place_kernel,
        grid=(4,),
        out_shape=jax.ShapeDtypeStruct((GCAP, L, width), jnp.bfloat16),
        in_specs=[pl.BlockSpec((shards * GCAP, width), lambda g: (0, g))],
        out_specs=pl.BlockSpec((GCAP, 32, width), lambda g: (0, g, 0)),
        scratch_shapes=[pltpu.VMEM((width // HD, shards * GCAP, HD), jnp.float32)],
        compiler_params=pltpu.CompilerParams(vmem_limit_bytes=40 * 2**20),
    )(arrived.reshape(shards * GCAP, 4 * width))


def solution(mesh):
    placed = (
        P("dp", None),
        P("dp", None),
        P("dp", None, "mp"),
        P("dp", None, "mp"),
        P(None, "mp"),
        P(None, "mp"),
        P(None, "mp"),
    )
    return jax.shard_map(on_device, mesh=mesh, in_specs=placed, out_specs=P("dp", None, "mp"), check_vma=False)
```
